512 devices in a mesh: pipe: 64 (over x_lo, z, core), tp: 8 (over x_hi, y).
Axes of the slice: x: 4 (x_hi: 2, x_lo: 2; x = x_hi * 2 + x_lo), y: 4, z: 16, core: 2. Of those that a mesh axis runs over, the one named last changes fastest.
Arguments:
- carried: bfloat16 [64, 256, 4096], P('pipe', None, 'tp'), may hold values from -8 to 8
- fresh: bfloat16 [2, 256, 4096], P(None, None, 'tp'), may hold values from -8 to 8
- gains: bfloat16 [64, 4096], P('pipe', 'tp'), may hold values from 0.25 to 1.75
- qkv_weight: bfloat16 [64, 4096, 2304], P('pipe', 'tp'), may hold values from -1 to 1
- out_weight: bfloat16 [64, 2048, 4096], P('pipe', None, 'tp'), may hold values from -0.125 to 0.125
- segments: int32 [66, 256], replicated, may hold values from 0 to 15, never falling along the last dimension, each value on 1 to 128 neighbouring positions
- evict_tick: int32 [64], P('pipe'), may hold values from 0 to 2
Outputs:
- section_out: bfloat16 [64, 256, 4096], P('pipe', None, 'tp')
- evicted: bfloat16 [64, 256, 4096], P('pipe', None, 'tp')
The draws below stay inside these ranges and needn't reach their ends.
Inputs may be any that keep to these rules, and one draw needn't show every extreme that they name: `segments`: segment ids never fall along a row.
All inputs are finite; a program needn't handle non-finite values.
Results may differ from the reference program's by a relative error of at most 0.015.
Values may be sent and summed in bfloat16 or wider, within the bound.
No kernel may reach another device: no remote copies, remote signals or barrier semaphores. Data moves between devices by JAX's collectives and lax.ppermute only.
A program may use at most 64 MiB of HBM per device.

```python
import math
import jax
import jax.numpy as jnp
import numpy as np
from jax import lax

MODEL_DIM = 4096
HEAD_DIM = 128
KV_HEADS = 1
MB_TOKENS = 256
WINDOW_TICKS = 3
SECTIONS = 64
MICRO_ITEMS = 66
Q_HEADS = 16
PROJ_COLS = 2304


def draw_carried(key, part):
    key = jax.random.fold_in(key, 11)
    noise_key = jax.random.fold_in(key, 0)
    full_shape = (SECTIONS, MB_TOKENS, MODEL_DIM)
    values = jax.random.truncated_normal(noise_key, -6.0, 6.0, full_shape, jnp.float32)
    return values.astype(jnp.bfloat16)


def draw_fresh(key, part):
    key = jax.random.fold_in(key, 12)
    noise_key = jax.random.fold_in(key, 0)
    full_shape = (WINDOW_TICKS - 1, MB_TOKENS, MODEL_DIM)
    values = jax.random.truncated_normal(noise_key, -6.0, 6.0, full_shape, jnp.float32)
    return values.astype(jnp.bfloat16)


def draw_qkv_weight(key, part):
    key = jax.random.fold_in(key, 13)
    noise_key = jax.random.fold_in(key, 0)
    full_shape = (SECTIONS, MODEL_DIM, PROJ_COLS)
    weights = jax.random.truncated_normal(noise_key, -4.0, 4.0, full_shape, jnp.float32) * MODEL_DIM ** (-0.5)
    return weights.astype(jnp.bfloat16)


def touch_ends(entries, key, least, high):
    longest = entries.shape.index(max(entries.shape))
    spots = []
    for shift in (0, 1):
        where = [jax.random.randint(jax.random.fold_in(key, axis), (), 0, length) for axis, length in enumerate(entries.shape)]
        where[longest] = (where[longest] + shift) % entries.shape[longest]
        spots.append(tuple(where))
    return entries.at[spots[0]].set(least).at[spots[1]].set(high)


def level_of(rng, extent, pieces, low, high):
    factor_of, own = 1.0, jax.random.fold_in(rng, 6)
    for axis_at, blocks in pieces:
        steps = jnp.exp(jax.random.uniform(jax.random.fold_in(own, axis_at), (blocks,), jnp.float32, low / len(pieces), high / len(pieces)))
        factor_of = factor_of * jnp.repeat(steps, extent[axis_at] // blocks).reshape([-1 if axis == axis_at else 1 for axis in range(len(extent))])
    return factor_of


def length_profile(count, total, reach, skew):
    portions = [(1 << 20) // math.isqrt(grade ** skew) + 1 for grade in range(2, count + 1)]
    rest, holding = total - reach - (count - 1), [1] * (count - 1)
    while rest > 0:
        free = [i for i in range(count - 1) if holding[i] < reach]
        pool, remaining = sum([portions[i] for i in free]), rest
        for i in free:
            more = min(reach - holding[i], max(1, remaining * portions[i] // pool), rest)
            holding[i] = holding[i] + more
            rest = rest - more
    return np.array([reach] + holding)


def ragged_sizes(own_key, count, total, most, skew):
    if count == 2:
        one = jax.random.randint(own_key, (), max(1, total - most), min(most, total - 1) + 1)
        return jnp.stack([one, total - one])
    lengths = jnp.asarray(length_profile(count, total, most, skew), jnp.int32)
    pairs = (count - 1) // 2
    source_of, taker = lengths[1:1 + 2 * pairs:2], lengths[2:2 + 2 * pairs:2]
    margin = jnp.minimum(source_of - 1, most - taker)
    passed = jax.random.randint(jax.random.fold_in(own_key, 1), (pairs,), 0, 1 << 20) % (margin + 1)
    lengths = lengths.at[1:1 + 2 * pairs:2].set(source_of - passed).at[2:2 + 2 * pairs:2].set(taker + passed)
    return lengths[jax.random.permutation(jax.random.fold_in(own_key, 2), count)]


def gaussian(key, shape, spread, reach, cuts=(), held_as=jnp.bfloat16):
    factor_of = level_of(key, shape, cuts, -0.22, 0.18) if cuts else 1.0
    drawn = jax.random.normal(key, shape, jnp.float32) * spread * factor_of
    return jnp.minimum(jnp.maximum(drawn, -reach), reach).astype(held_as)


def setup_inputs(seed: int = 0) -> dict:
    key_of = jax.random.split(jax.random.key(seed), 8)
    return {
        "carried": draw_carried(jax.random.fold_in(key_of[7], 71), 0),
        "fresh": draw_fresh(jax.random.fold_in(key_of[7], 71), 0),
        "gains": jnp.clip(1.0 + 0.15 * jax.random.normal(key_of[2], (SECTIONS, MODEL_DIM), jnp.float32), 0.25, 1.75).astype(jnp.bfloat16),
        "qkv_weight": draw_qkv_weight(jax.random.fold_in(key_of[7], 71), 0),
        "out_weight": gaussian(key_of[4], (SECTIONS, Q_HEADS * HEAD_DIM, MODEL_DIM), (Q_HEADS * HEAD_DIM) ** -0.5, 0.125, ((0, 64), (2, 8))),
        "segments": jax.vmap(lambda own: jnp.searchsorted(jnp.cumsum(ragged_sizes(own, max(4, MB_TOKENS // 16), MB_TOKENS, MB_TOKENS // 2, 2)), jnp.arange(MB_TOKENS), side="right"))(jax.random.split(key_of[5], MICRO_ITEMS)).reshape((MICRO_ITEMS, MB_TOKENS)).astype(jnp.int32),
        "evict_tick": touch_ends(jax.random.randint(key_of[6], (SECTIONS,), 0, WINDOW_TICKS), jax.random.fold_in(key_of[6], 1), 0, WINDOW_TICKS - 1).astype(jnp.int32),
    }


norm_eps = 1e-05

def attend(queries, keys, values, query_pos, key_pos, query_seg, key_seg):
    row_count = queries.shape[0]
    length = keys.shape[0]
    kv_count = keys.shape[1] // HEAD_DIM
    group_size = queries.shape[1] // HEAD_DIM // kv_count
    query_blocks = queries.reshape(row_count, kv_count, group_size, HEAD_DIM).astype(jnp.float32)
    key_blocks = keys.reshape(length, kv_count, HEAD_DIM).astype(jnp.float32)
    value_blocks = values.reshape(length, kv_count, HEAD_DIM).astype(jnp.float32)
    scores = jnp.einsum('rkgd,tkd->kgrt', query_blocks, key_blocks) * HEAD_DIM ** (-0.5)
    visible = (query_seg[:, None] == key_seg[None, :]) & (query_pos[:, None] >= key_pos[None, :])
    scores = jnp.where(visible, scores, jnp.float32(-1e+30))
    highest = lax.optimization_barrier(jnp.max(scores, axis=-1, keepdims=True))
    exponentials = jnp.where(visible, jnp.exp(scores - highest), jnp.float32(0.0))
    totals = lax.optimization_barrier(jnp.sum(exponentials, axis=-1, keepdims=True))
    attention = (exponentials / totals).astype(jnp.bfloat16)
    mixed = jnp.einsum('kgrt,tkd->rkgd', attention.astype(jnp.float32), value_blocks)
    return mixed.reshape(row_count, kv_count * group_size * HEAD_DIM).astype(jnp.bfloat16)

def layer(current, gain, qkv_weight, out_weight, section_segments):
    wide_input = current.astype(jnp.float32)
    square_sums = lax.optimization_barrier(jnp.sum(wide_input * wide_input, axis=1))
    scale = lax.rsqrt(square_sums / MODEL_DIM + norm_eps)
    normed = (wide_input * scale[:, None] * gain.astype(jnp.float32)).astype(jnp.bfloat16)
    projected = jnp.dot(normed, qkv_weight, preferred_element_type=jnp.float32).astype(jnp.bfloat16)
    query_width = Q_HEADS * HEAD_DIM
    key_width = KV_HEADS * HEAD_DIM
    positions = jnp.arange(current.shape[0], dtype=jnp.int32)
    mixed = attend(projected[:, :query_width], projected[:, query_width:query_width + key_width], projected[:, query_width + key_width:], positions, positions, section_segments, section_segments)
    return (wide_input + jnp.dot(mixed, out_weight, preferred_element_type=jnp.float32)).astype(jnp.bfloat16)

def reference(carried, fresh, gains, qkv_weight, out_weight, segments, evict_tick):
    inputs = carried
    chosen = jnp.zeros_like(carried)
    outputs = carried
    for tick_index in range(WINDOW_TICKS):
        if tick_index > 0:
            inputs = jnp.concatenate([fresh[tick_index - 1][None], outputs[:-1]], axis=0)
        first_row = WINDOW_TICKS - 1 - tick_index
        section_segments = segments[first_row:first_row + SECTIONS]
        chosen = jnp.where((evict_tick == tick_index)[:, None, None], inputs, chosen)
        outputs = lax.map(lambda packed: layer(*packed), (inputs, gains, qkv_weight, out_weight, section_segments))
    flipped = chosen[::-1]
    receiving = jnp.arange(SECTIONS, dtype=jnp.int32) >= SECTIONS // 2
    evicted = jnp.where(receiving[:, None, None], flipped, jnp.zeros_like(flipped))
    return (outputs, evicted)
```

```python
import functools

import jax
import jax.numpy as jnp
from jax import lax
from jax.experimental import pallas as pl
from jax.experimental.pallas import tpu as pltpu
from jax.sharding import PartitionSpec as P

HEAD_DIM = 128
Q_HEADS = 16
Q_COLS = Q_HEADS * HEAD_DIM
KV_COLS = 2 * HEAD_DIM
LONGEST_SEGMENT = 128
NORM_EPS = 1e-05
F32 = jnp.float32
BF16 = jnp.bfloat16


def window_blocks(rows):
    return (LONGEST_SEGMENT + rows - 2) // rows + 1


def project_kernel(parts, x_ref, gain_ref, weight_ref, out_ref):
    tokens = x_ref.shape[0]
    rows = tokens // parts
    blocks = window_blocks(rows)
    wide = x_ref[...].astype(F32)
    scaled = (wide * gain_ref[...].astype(F32)).astype(BF16)
    squares = jnp.sum(wide * wide, axis=1, keepdims=True)
    high = squares.astype(BF16).astype(F32)
    low = squares - high
    lane = lax.broadcasted_iota(jnp.int32, (rows, 128), 1)
    step = 256
    for start in range(0, Q_COLS, step):
        tile = jnp.dot(scaled, weight_ref[:, start : start + step], preferred_element_type=F32)
        out_ref[:, :, start : start + step] = tile.astype(BF16).reshape(parts, rows, step)
    tile = jnp.dot(scaled, weight_ref[:, Q_COLS:], preferred_element_type=F32).astype(BF16)
    last = Q_COLS + blocks * KV_COLS
    for j in range(parts):
        sums = jnp.zeros((rows, 128), F32)
        for b in range(blocks):
            at = max(j - blocks + 1 + b, 0) * rows
            start = Q_COLS + b * KV_COLS
            out_ref[j, :, start : start + KV_COLS] = tile[at : at + rows]
            sums = jnp.where(lane == 2 * b, high[at : at + rows], sums)
            sums = jnp.where(lane == 2 * b + 1, low[at : at + rows], sums)
        out_ref[j, :, last:] = sums.astype(BF16)


def attend_kernel(parts, width, place_ref, segments_ref, got_ref, out_ref):
    rows = got_ref.shape[1]
    tokens = rows * parts
    blocks = window_blocks(rows)
    span = blocks * rows
    before = span - rows
    rank = place_ref[0]
    item = place_ref[1]

    def total(start, size):
        value = got_ref[0, :, start : start + size].astype(F32)
        for j in range(1, parts):
            value = value + got_ref[j, :, start : start + size].astype(F32)
        return value

    last = Q_COLS + blocks * KV_COLS
    sums = total(last, 128)
    scales = []
    for b in range(blocks):
        squares = sums[:, 2 * b : 2 * b + 1] + sums[:, 2 * b + 1 : 2 * b + 2]
        scales.append(lax.rsqrt(squares / width + NORM_EPS))
    keys, values = [], []
    for b in range(blocks):
        both = (total(Q_COLS + b * KV_COLS, KV_COLS) * scales[b]).astype(BF16)
        keys.append(both[:, :HEAD_DIM])
        values.append(both[:, HEAD_DIM:])
    keys = jnp.concatenate(keys, axis=0)
    values = jnp.concatenate(values, axis=0)
    queries = []
    for h in range(Q_HEADS):
        queries.append((total(h * HEAD_DIM, HEAD_DIM) * scales[-1]).astype(BF16))
    queries = jnp.concatenate(queries, axis=0)

    first = rank * rows - before
    segment_row = segments_ref[pl.ds(item, 1), :]
    segment_row = pltpu.roll(segment_row, lax.rem(tokens - first, tokens), 1)
    segment_rows = jnp.broadcast_to(segment_row, (rows, tokens))
    column = lax.broadcasted_iota(jnp.int32, (rows, tokens), 1)
    own = lax.broadcasted_iota(jnp.int32, (rows, tokens), 0) + before
    own_segment = jnp.sum(jnp.where(column == own, segment_rows, 0), axis=1, keepdims=True)
    visible = (segment_rows == own_segment) & (column <= own) & (column + first >= 0)
    visible = visible[:, :span]

    scores = lax.dot_general(
        queries, keys, (((1,), (1,)), ((), ())), preferred_element_type=F32
    ) * HEAD_DIM ** (-0.5)
    scores = scores.reshape(Q_HEADS, rows, span)
    scores = jnp.where(visible[None], scores, F32(-1e30))
    highest = jnp.max(scores, axis=-1, keepdims=True)
    exponentials = jnp.where(visible[None], jnp.exp(scores - highest), F32(0.0))
    totals = jnp.sum(exponentials, axis=-1, keepdims=True)
    attention = (exponentials / totals).astype(BF16).reshape(Q_HEADS * rows, span)
    mixed = jnp.dot(attention, values, preferred_element_type=F32).astype(BF16)
    for h in range(Q_HEADS):
        piece = mixed[h * rows : (h + 1) * rows]
        for j in range(parts):
            out_ref[j, :, h * HEAD_DIM : (h + 1) * HEAD_DIM] = piece


def output_kernel(x_ref, mixed_ref, weight_ref, out_ref):
    product = jnp.dot(mixed_ref[...], weight_ref[...], preferred_element_type=F32)
    out_ref[...] = (x_ref[...].astype(F32) + product).astype(BF16)


VMEM = pl.BlockSpec(memory_space=pltpu.VMEM)
SMEM = pl.BlockSpec(memory_space=pltpu.SMEM)
PARAMS = pltpu.CompilerParams(vmem_limit_bytes=24 * 1024 * 1024)


def section_layer(current, gain, qkv_weight, out_weight, segments, place):
    parts = lax.axis_size("tp")
    tokens, width = current.shape
    rows = tokens // parts
    columns = Q_COLS + window_blocks(rows) * KV_COLS + 128
    partial_proj = pl.pallas_call(
        functools.partial(project_kernel, parts),
        out_shape=jax.ShapeDtypeStruct((parts, rows, columns), BF16),
        in_specs=[VMEM] * 3,
        out_specs=VMEM,
        compiler_params=PARAMS,
        name="project",
    )(current, gain, qkv_weight)
    got = lax.all_to_all(partial_proj, "tp", split_axis=0, concat_axis=0, tiled=True)
    mixed = pl.pallas_call(
        functools.partial(attend_kernel, parts, width * parts),
        out_shape=jax.ShapeDtypeStruct((parts, rows, Q_COLS), BF16),
        in_specs=[SMEM, VMEM, VMEM],
        out_specs=VMEM,
        compiler_params=PARAMS,
        name="attend",
    )(place, segments, got)
    mixed = lax.all_to_all(mixed, "tp", split_axis=0, concat_axis=0, tiled=True)
    return pl.pallas_call(
        output_kernel,
        out_shape=jax.ShapeDtypeStruct((tokens, width), BF16),
        in_specs=[VMEM] * 3,
        out_specs=VMEM,
        compiler_params=PARAMS,
        name="project_out",
    )(current, mixed.reshape(tokens, Q_COLS), out_weight)


def shards(carried, fresh, gains, qkv_weight, out_weight, segments, evict_tick):
    section = lax.axis_index("pipe")
    rank = lax.axis_index("tp")
    sections = lax.axis_size("pipe")
    ticks = fresh.shape[0] + 1
    current = carried[0]
    chosen = current
    result = current
    for tick in range(ticks):
        if tick > 0:
            pairs = [(i, i + 1) for i in range(sections - 1)]
            arrived = lax.ppermute(result, "pipe", pairs)
            current = jnp.where(section == 0, fresh[tick - 1], arrived)
            chosen = jnp.where(evict_tick[0] == tick, current, chosen)
        place = jnp.stack([rank, section - tick + ticks - 1]).astype(jnp.int32)
        result = section_layer(current, gains, qkv_weight[0], out_weight[0], segments, place)
    pairs = [(i, sections - 1 - i) for i in range(sections // 2)]
    evicted = lax.ppermute(chosen, "pipe", pairs)
    return (result[None], evicted[None])


def solution(mesh):
    placed = (
        P("pipe", None, "tp"),
        P(None, None, "tp"),
        P("pipe", "tp"),
        P("pipe", "tp", None),
        P("pipe", None, "tp"),
        P(),
        P("pipe"),
    )
    return jax.shard_map(
        shards,
        mesh=mesh,
        in_specs=placed,
        out_specs=(P("pipe", None, "tp"), P("pipe", None, "tp")),
        check_vma=False,
    )
```

```python
import functools

import jax
import jax.numpy as jnp
from jax import lax
from jax.experimental import pallas as pl
from jax.experimental.pallas import tpu as pltpu
from jax.sharding import PartitionSpec as P

HEAD_DIM = 128
Q_HEADS = 16
Q_COLS = Q_HEADS * HEAD_DIM
KV_COLS = 2 * HEAD_DIM
LONGEST_SEGMENT = 128
NORM_EPS = 1e-05
F32 = jnp.float32
BF16 = jnp.bfloat16


def window_blocks(rows):
    return (LONGEST_SEGMENT + rows - 2) // rows + 1


def project_rows(parts, wide, scaled, weight_ref, out_ref):
    rows = wide.shape[0] // parts
    blocks = window_blocks(rows)
    squares = jnp.sum(wide * wide, axis=1, keepdims=True)
    high = squares.astype(BF16).astype(F32)
    low = squares - high
    lane = lax.broadcasted_iota(jnp.int32, (rows, 128), 1)
    step = 256
    for start in range(0, Q_COLS, step):
        tile = jnp.dot(scaled, weight_ref[:, start : start + step], preferred_element_type=F32)
        out_ref[:, :, start : start + step] = tile.astype(BF16).reshape(parts, rows, step)
    tile = jnp.dot(scaled, weight_ref[:, Q_COLS:], preferred_element_type=F32).astype(BF16)
    last = Q_COLS + blocks * KV_COLS
    for j in range(parts):
        sums = jnp.zeros((rows, 128), F32)
        for b in range(blocks):
            at = max(j - blocks + 1 + b, 0) * rows
            start = Q_COLS + b * KV_COLS
            out_ref[j, :, start : start + KV_COLS] = tile[at : at + rows]
            sums = jnp.where(lane == 2 * b, high[at : at + rows], sums)
            sums = jnp.where(lane == 2 * b + 1, low[at : at + rows], sums)
        out_ref[j, :, last:] = sums.astype(BF16)


def project_kernel(parts, tick, stash, flags_ref, *refs):
    earlier, refs = (refs[:tick], refs[tick:]) if stash else ((), refs)
    if tick > 0:
        arrived_ref, fresh_ref, gain_ref, weight_ref, out_ref, current_ref = refs[:6]
        current = jnp.where(flags_ref[0] == 1, fresh_ref[tick - 1], arrived_ref[...])
        current_ref[...] = current
    else:
        arrived_ref, gain_ref, weight_ref, out_ref = refs
        current = arrived_ref[...]
    if earlier:
        chosen = current
        for at, earlier_ref in enumerate(earlier):
            chosen = jnp.where(flags_ref[1] == at, earlier_ref[...], chosen)
        half = chosen.shape[0] // 2
        refs[6][...] = chosen[:half]
        refs[7][...] = chosen[half:]
    wide = current.astype(F32)
    scaled = (wide * gain_ref[...].astype(F32)).astype(BF16)
    project_rows(parts, wide, scaled, weight_ref, out_ref)


def attend_kernel(parts, width, place_ref, segments_ref, got_ref, *refs):
    out_ref = refs[-1]
    rows = got_ref.shape[1]
    tokens = rows * parts
    blocks = window_blocks(rows)
    span = blocks * rows
    before = span - rows
    rank = place_ref[0]
    item = place_ref[1]

    def total(start, size):
        value = got_ref[0, :, start : start + size].astype(F32)
        for j in range(1, parts):
            value = value + got_ref[j, :, start : start + size].astype(F32)
        return value

    last = Q_COLS + blocks * KV_COLS
    sums = total(last, 128)
    scales = []
    for b in range(blocks):
        squares = sums[:, 2 * b : 2 * b + 1] + sums[:, 2 * b + 1 : 2 * b + 2]
        scales.append(lax.rsqrt(squares / width + NORM_EPS))
    keys, values = [], []
    for b in range(blocks):
        both = (total(Q_COLS + b * KV_COLS, KV_COLS) * scales[b]).astype(BF16)
        keys.append(both[:, :HEAD_DIM])
        values.append(both[:, HEAD_DIM:])
    keys = jnp.concatenate(keys, axis=0)
    values = jnp.concatenate(values, axis=0)
    queries = []
    for h in range(Q_HEADS):
        queries.append((total(h * HEAD_DIM, HEAD_DIM) * scales[-1]).astype(BF16))
    queries = jnp.concatenate(queries, axis=0)

    first = rank * rows - before
    segment_row = segments_ref[pl.ds(item, 1), :]
    segment_row = pltpu.roll(segment_row, lax.rem(tokens - first, tokens), 1)
    segment_rows = jnp.broadcast_to(segment_row, (rows, tokens))
    column = lax.broadcasted_iota(jnp.int32, (rows, tokens), 1)
    own = lax.broadcasted_iota(jnp.int32, (rows, tokens), 0) + before
    own_segment = jnp.sum(jnp.where(column == own, segment_rows, 0), axis=1, keepdims=True)
    visible = (segment_rows == own_segment) & (column <= own) & (column + first >= 0)
    visible = visible[:, :span]

    scores = lax.dot_general(
        queries, keys, (((1,), (1,)), ((), ())), preferred_element_type=F32
    ) * HEAD_DIM ** (-0.5)
    scores = scores.reshape(Q_HEADS, rows, span)
    scores = jnp.where(visible[None], scores, F32(-1e30))
    highest = jnp.max(scores, axis=-1, keepdims=True)
    exponentials = jnp.where(visible[None], jnp.exp(scores - highest), F32(0.0))
    totals = jnp.sum(exponentials, axis=-1, keepdims=True)
    attention = (exponentials / totals).astype(BF16).reshape(Q_HEADS * rows, span)
    mixed = jnp.dot(attention, values, preferred_element_type=F32).astype(BF16)
    for h in range(Q_HEADS):
        piece = mixed[h * rows : (h + 1) * rows]
        for j in range(parts):
            out_ref[j, :, h * HEAD_DIM : (h + 1) * HEAD_DIM] = piece


def output_kernel(x_ref, mixed_ref, weight_ref, out_ref):
    product = jnp.dot(mixed_ref[...], weight_ref[...], preferred_element_type=F32)
    out_ref[...] = (x_ref[...].astype(F32) + product).astype(BF16)


VMEM = pl.BlockSpec(memory_space=pltpu.VMEM)
SMEM = pl.BlockSpec(memory_space=pltpu.SMEM)
ANY = pl.BlockSpec(memory_space=pl.ANY)
PARAMS = pltpu.CompilerParams(vmem_limit_bytes=24 * 1024 * 1024)


def shard(shape):
    return jax.ShapeDtypeStruct(shape, BF16)


def exchange(value):
    return lax.all_to_all(value, "tp", split_axis=0, concat_axis=0, tiled=True)


def attend(place, segments, got, width, waited=()):
    parts, rows, _ = got.shape
    return pl.pallas_call(
        functools.partial(attend_kernel, parts, width),
        out_shape=shard((parts, rows, Q_COLS)),
        in_specs=[SMEM, VMEM, VMEM] + [ANY] * len(waited),
        out_specs=VMEM,
        compiler_params=PARAMS,
        name="attend",
    )(place, segments, got, *waited)


def project_out(current, mixed, out_weight):
    return pl.pallas_call(
        output_kernel,
        out_shape=shard(current.shape),
        in_specs=[VMEM] * 3,
        out_specs=VMEM,
        compiler_params=PARAMS,
        name="project_out",
    )(current, mixed.reshape(current.shape[0], Q_COLS), out_weight)


def shards(carried, fresh, gains, qkv_weight, out_weight, segments, evict_tick):
    section = lax.axis_index("pipe")
    rank = lax.axis_index("tp")
    sections = lax.axis_size("pipe")
    parts = lax.axis_size("tp")
    ticks = fresh.shape[0] + 1
    tokens, width = carried.shape[1:]
    rows = tokens // parts
    columns = Q_COLS + window_blocks(rows) * KV_COLS + 128
    flags = jnp.stack([(section == 0).astype(jnp.int32), evict_tick[0]])
    following = [(i, i + 1) for i in range(sections - 1)]
    half = sections // 2
    across = [(i, i + half) for i in range(half)]
    turned = [(i, half - 1 - i) for i in range(half)]
    turned_across = [(half + i, sections - 1 - i) for i in range(half)]
    inputs = [carried[0]]
    for tick in range(ticks):
        outs = [shard((parts, rows, columns))]
        operands = [flags, inputs[0], gains, qkv_weight[0]]
        specs = [SMEM, VMEM, VMEM, VMEM]
        if tick > 0:
            arrived = lax.ppermute(result, "pipe", following)
            operands = [flags, arrived, fresh, gains, qkv_weight[0]]
            specs = [SMEM, VMEM, VMEM, VMEM, VMEM]
            outs.append(shard((tokens, width)))
        if tick == ticks - 1:
            operands[1:1] = inputs
            specs[1:1] = [VMEM] * tick
            outs += [shard((tokens // 2, width))] * 2
        got = pl.pallas_call(
            functools.partial(project_kernel, parts, tick, tick == ticks - 1),
            out_shape=outs,
            in_specs=specs,
            out_specs=[VMEM] * len(outs),
            compiler_params=PARAMS,
            name="project",
        )(*operands)
        partial_proj = got[0]
        if tick > 0:
            inputs.append(got[1])
        sums = exchange(partial_proj)
        place = jnp.stack([rank, section - tick + ticks - 1]).astype(jnp.int32)
        waited = ()
        if tick == ticks - 1:
            waited = (lax.ppermute(got[2], "pipe", across), lax.ppermute(got[3], "pipe", turned))
        mixed = exchange(attend(place, segments, sums, width * parts, waited))
        result = project_out(inputs[tick], mixed, out_weight[0])
    top = lax.ppermute(waited[0], "pipe", turned_across)
    low = lax.ppermute(waited[1], "pipe", across)
    evicted = jnp.concatenate([top, low], axis=0)
    return (result[None], evicted[None])


def solution(mesh):
    placed = (
        P("pipe", None, "tp"),
        P(None, None, "tp"),
        P("pipe", "tp"),
        P("pipe", "tp", None),
        P("pipe", None, "tp"),
        P(),
        P("pipe"),
    )
    return jax.shard_map(
        shards,
        mesh=mesh,
        in_specs=placed,
        out_specs=(P("pipe", None, "tp"), P("pipe", None, "tp")),
        check_vma=False,
    )
```

```python
import functools

import jax
import jax.numpy as jnp
from jax import lax
from jax.experimental import pallas as pl
from jax.experimental.pallas import tpu as pltpu
from jax.sharding import PartitionSpec as P

HEAD_DIM = 128
Q_HEADS = 16
Q_COLS = Q_HEADS * HEAD_DIM
HALF_COLS = Q_COLS // 2
KV_COLS = 2 * HEAD_DIM
LONGEST_SEGMENT = 128
NORM_EPS = 1e-05
STEP = 256
GAIN_ROWS = 16
F32 = jnp.float32
BF16 = jnp.bfloat16

RANK, HALF, SECTION, LAST, EVICT = range(5)


def window_blocks(rows):
    return (LONGEST_SEGMENT + rows - 2) // rows + 1


def put_sums(high_low, rows):
    lane = lax.broadcasted_iota(jnp.int32, (rows, 128), 1)
    sums = jnp.zeros((rows, 128), F32)
    for b, squares in enumerate(high_low):
        high = squares.astype(BF16).astype(F32)
        sums = jnp.where(lane == 2 * b, high, sums)
        sums = jnp.where(lane == 2 * b + 1, squares - high, sums)
    return sums.astype(BF16)


def put_window(kv, squares, out_ref, start):
    parts, rows, _ = out_ref.shape
    blocks = window_blocks(rows)
    last = start + blocks * KV_COLS
    for j in range(parts):
        spots = [max(j - blocks + 1 + b, 0) * rows for b in range(blocks)]
        for b, at in enumerate(spots):
            out_ref[j, :, start + b * KV_COLS : start + (b + 1) * KV_COLS] = kv[at : at + rows]
        out_ref[j, :, last:] = put_sums([squares[at : at + rows] for at in spots], rows)


def scale_rows(x_ref, gain):
    wide = x_ref[...].astype(F32)
    squares = jnp.sum(wide * wide, axis=1, keepdims=True)
    return (wide * gain.astype(F32)).astype(BF16), squares


def dot(a, b):
    return jnp.dot(a, b, preferred_element_type=F32)


def project_first_kernel(x_ref, gain_ref, weight_ref, out_ref):
    parts, rows, _ = out_ref.shape
    scaled, squares = scale_rows(x_ref, gain_ref[...])
    for start in range(0, Q_COLS, STEP):
        tile = dot(scaled, weight_ref[:, start : start + STEP]).astype(BF16)
        out_ref[:, :, start : start + STEP] = tile.reshape(parts, rows, STEP)
    kv = dot(scaled, weight_ref[:, Q_COLS:]).astype(BF16)
    put_window(kv, squares, out_ref, Q_COLS)


def project_kernel(stash, place_ref, own_ref, other_ref, gain_ref, weight_ref, first_ref, second_ref, *refs):
    if stash:
        earlier, (out_ref, top_ref, low_ref) = refs[:-3], refs[-3:]
        chosen = own_ref[...]
        for at, earlier_ref in enumerate(earlier):
            chosen = jnp.where(place_ref[EVICT] == at, earlier_ref[...], chosen)
        middle = chosen.shape[0] // 2
        top_ref[...] = chosen[:middle]
        low_ref[...] = chosen[middle:]
    else:
        (out_ref,) = refs
    parts, rows, _ = out_ref.shape
    depth = second_ref.shape[0]
    width = own_ref.shape[1]
    own, own_squares = scale_rows(own_ref, gain_ref[...])
    other, other_squares = scale_rows(other_ref, first_ref[depth : depth + 1, :width])
    squares = own_squares + other_squares

    def tile(columns, at):
        total = dot(own, weight_ref[:, columns])
        total = total + dot(other[:, :depth], first_ref[:depth, at : at + STEP])
        return (total + dot(other[:, depth:], second_ref[:, at : at + STEP])).astype(BF16)

    half = place_ref[HALF] * HALF_COLS
    for start in range(0, HALF_COLS, STEP):
        queries = tile(pl.ds(pl.multiple_of(half + start, STEP), STEP), start)
        out_ref[:, :, start : start + STEP] = queries.reshape(parts, rows, STEP)
    kv = tile(slice(Q_COLS, Q_COLS + KV_COLS), HALF_COLS)
    put_window(kv, squares, out_ref, HALF_COLS)


def share_kernel(begin, gain_rows, place_ref, gain_ref, weight_ref, *refs):
    out_ref = refs[-1]
    depth = out_ref.shape[0] - gain_rows
    half = pl.multiple_of((1 - place_ref[HALF]) * HALF_COLS, HALF_COLS)
    out_ref[:depth, :HALF_COLS] = weight_ref[begin : begin + depth, pl.ds(half, HALF_COLS)]
    out_ref[:depth, HALF_COLS:] = weight_ref[begin : begin + depth, Q_COLS:]
    if gain_rows:
        width = gain_ref.shape[1]
        out_ref[depth:, :width] = jnp.broadcast_to(gain_ref[...], (gain_rows, width))
        out_ref[depth:, width:] = jnp.zeros((gain_rows, out_ref.shape[1] - width), BF16)


def fold_kernel(place_ref, got_ref, waited_ref, keep_ref, send_ref):
    parts, rows, _ = got_ref.shape
    blocks = window_blocks(rows)

    def total(columns):
        value = got_ref[0, :, columns].astype(F32)
        for j in range(1, parts):
            value = value + got_ref[j, :, columns].astype(F32)
        return value

    own = place_ref[HALF] * HALF_COLS
    other = HALF_COLS - own
    for start in range(0, HALF_COLS, STEP):
        columns = slice(start, start + STEP)
        keep_ref[0, :, columns] = total(pl.ds(pl.multiple_of(own + start, STEP), STEP)).astype(BF16)
        send_ref[0, :, columns] = total(pl.ds(pl.multiple_of(other + start, STEP), STEP)).astype(BF16)
    span = blocks * KV_COLS
    window = total(slice(Q_COLS, Q_COLS + span)).astype(BF16)
    sums = total(slice(Q_COLS + span, Q_COLS + span + 128))
    sums = put_sums([sums[:, 2 * b : 2 * b + 1] + sums[:, 2 * b + 1 : 2 * b + 2] for b in range(blocks)], rows)
    for ref in (keep_ref, send_ref):
        ref[0, :, HALF_COLS : HALF_COLS + span] = window
        ref[0, :, HALF_COLS + span :] = sums


def attend_kernel(tick, ticks, parts, width, partials, place_ref, segments_ref, *refs):
    out_ref = refs[-1]
    copies, rows, columns = out_ref.shape
    heads = columns // HEAD_DIM
    tokens = rows * parts
    blocks = window_blocks(rows)
    span = blocks * rows
    before = span - rows

    def total(start, size):
        value = None
        for ref in refs[:partials]:
            for j in range(ref.shape[0]):
                piece = ref[j, :, start : start + size].astype(F32)
                value = piece if value is None else value + piece
        return value

    sums = total(columns + blocks * KV_COLS, 128)
    scales = []
    for b in range(blocks):
        squares = sums[:, 2 * b : 2 * b + 1] + sums[:, 2 * b + 1 : 2 * b + 2]
        scales.append(lax.rsqrt(squares / width + NORM_EPS))
    keys, values = [], []
    for b in range(blocks):
        both = (total(columns + b * KV_COLS, KV_COLS) * scales[b]).astype(BF16)
        keys.append(both[:, :HEAD_DIM])
        values.append(both[:, HEAD_DIM:])
    keys = jnp.concatenate(keys, axis=0)
    values = jnp.concatenate(values, axis=0)
    queries = []
    for h in range(heads):
        queries.append((total(h * HEAD_DIM, HEAD_DIM) * scales[-1]).astype(BF16))
    queries = jnp.concatenate(queries, axis=0)

    first = place_ref[RANK] * rows - before
    item = place_ref[SECTION] + (ticks - 1 - tick)
    segment_row = segments_ref[pl.ds(item, 1), :]
    segment_row = pltpu.roll(segment_row, lax.rem(tokens - first, tokens), 1)
    segment_rows = jnp.broadcast_to(segment_row, (rows, tokens))
    column = lax.broadcasted_iota(jnp.int32, (rows, tokens), 1)
    own = lax.broadcasted_iota(jnp.int32, (rows, tokens), 0) + before
    own_segment = jnp.sum(jnp.where(column == own, segment_rows, 0), axis=1, keepdims=True)
    visible = (segment_rows == own_segment) & (column <= own) & (column + first >= 0)
    visible = visible[:, :span]

    scores = lax.dot_general(
        queries, keys, (((1,), (1,)), ((), ())), preferred_element_type=F32
    ) * HEAD_DIM ** (-0.5)
    scores = scores.reshape(heads, rows, span)
    scores = jnp.where(visible[None], scores, F32(-1e30))
    highest = jnp.max(scores, axis=-1, keepdims=True)
    exponentials = jnp.where(visible[None], jnp.exp(scores - highest), F32(0.0))
    totals = jnp.sum(exponentials, axis=-1, keepdims=True)
    attention = (exponentials / totals).astype(BF16).reshape(heads * rows, span)
    mixed = dot(attention, values).astype(BF16)
    for h in range(heads):
        piece = mixed[h * rows : (h + 1) * rows]
        for j in range(copies):
            out_ref[j, :, h * HEAD_DIM : (h + 1) * HEAD_DIM] = piece


def join_kernel(place_ref, own_ref, other_ref, out_ref):
    own = pl.multiple_of(place_ref[HALF] * HALF_COLS, HALF_COLS)
    other = pl.multiple_of((1 - place_ref[HALF]) * HALF_COLS, HALF_COLS)
    for j in range(out_ref.shape[0]):
        out_ref[j, :, pl.ds(own, HALF_COLS)] = own_ref[0]
        out_ref[j, :, pl.ds(other, HALF_COLS)] = other_ref[0]


def output_kernel(tick, place_ref, x_ref, mixed_ref, weight_ref, *refs):
    out_ref = refs[-1]
    tokens = x_ref.shape[0]
    parts, rows, columns = mixed_ref.shape
    group = tokens // rows
    product = None
    for at in range(parts // group):
        mixed = mixed_ref[at * group : (at + 1) * group].reshape(tokens, columns)
        piece = dot(mixed, weight_ref[at * columns : (at + 1) * columns])
        product = piece if product is None else product + piece
    result = (x_ref[...].astype(F32) + product).astype(BF16)
    if tick is not None:
        result = jnp.where(place_ref[LAST] == 1, refs[0][tick], result)
    out_ref[...] = result


VMEM = pl.BlockSpec(memory_space=pltpu.VMEM)
SMEM = pl.BlockSpec(memory_space=pltpu.SMEM)
ANY = pl.BlockSpec(memory_space=pl.ANY)
PARAMS = pltpu.CompilerParams(vmem_limit_bytes=24 * 1024 * 1024)


def call(kernel, name, shapes, operands, waited=()):
    specs = [SMEM if value.ndim == 1 else VMEM for value in operands] + [ANY] * len(waited)
    outs = [jax.ShapeDtypeStruct(shape, BF16) for shape in shapes]
    got = pl.pallas_call(
        kernel,
        out_shape=outs,
        in_specs=specs,
        out_specs=[VMEM] * len(outs),
        compiler_params=PARAMS,
        name=name,
    )(*operands, *waited)
    return got if len(outs) > 1 else got[0]


def shards(carried, fresh, gains, qkv_weight, out_weight, segments, evict_tick):
    section = lax.axis_index("pipe")
    rank = lax.axis_index("tp")
    sections = lax.axis_size("pipe")
    parts = lax.axis_size("tp")
    group = parts // 2
    ticks = fresh.shape[0] + 1
    tokens, width = carried.shape[1:]
    rows = tokens // group
    tail = window_blocks(rows) * KV_COLS + 128
    qkv_weight, out_weight = qkv_weight[0], out_weight[0]
    place = jnp.stack(
        [rank % group, rank // group, section, (section == sections - 1).astype(jnp.int32), evict_tick[0]]
    )
    groups = [list(range(group)), list(range(group, parts))]
    partner = [(i, (i + group) % parts) for i in range(parts)]
    following = [(i, (i + 1) % sections) for i in range(sections)]
    crossing = [(i * parts + a, j * parts + b) for i, j in following for a, b in partner]
    half = sections // 2
    across = [(i, i + half) for i in range(half)]
    turned = [(i, half - 1 - i) for i in range(half)]
    turned_across = [(half + i, sections - 1 - i) for i in range(half)]

    def exchange(value, groups=None):
        return lax.all_to_all(value, "tp", split_axis=0, concat_axis=0, tiled=True, axis_index_groups=groups)

    def attend(tick, copies, sums, waited=()):
        kernel = functools.partial(attend_kernel, tick, ticks, group, width * parts, len(sums))
        shape = (copies, rows, HALF_COLS)
        return call(kernel, "attend", [shape], [place, segments, *sums], waited)

    def share(begin, depth, gain_rows, waited=()):
        kernel = functools.partial(share_kernel, begin, gain_rows)
        shape = (depth + gain_rows, HALF_COLS + KV_COLS)
        piece = call(kernel, "share", [shape], [place, gains, qkv_weight], waited)
        return lax.ppermute(piece, "tp", partner)

    own = carried[0]
    partial_proj = call(
        project_first_kernel, "project_first", [(group, rows, Q_COLS + tail)], [own, gains, qkv_weight]
    )
    first = share(0, width // 2, GAIN_ROWS, [partial_proj])
    sums = exchange(partial_proj, groups)
    keep, send = call(fold_kernel, "fold", [(1, rows, HALF_COLS + tail)] * 2, [place, sums], [first])
    mixed = attend(0, 1, [keep, lax.ppermute(send, "tp", partner)])
    arrived = lax.ppermute(mixed, "tp", partner)
    second = share(width // 2, width // 2, 0, [arrived])
    joined = call(join_kernel, "join", [(group, rows, Q_COLS)], [place, mixed, arrived])
    mixed = exchange(joined, groups)
    waited = (second,)
    inputs = [own]
    for tick in range(ticks):
        if tick > 0:
            other = lax.ppermute(result, ("pipe", "tp"), crossing)
            own = lax.ppermute(result, "pipe", following)
            stash = tick == ticks - 1
            operands = [place, own, other, gains, qkv_weight, first, second]
            shapes = [(group, rows, HALF_COLS + tail)]
            if stash:
                operands += inputs
                shapes += [(tokens // 2, width)] * 2
            got = call(functools.partial(project_kernel, stash), "project", shapes, operands)
            inputs.append(own)
            waited = ()
            if stash:
                got, top, low = got
                waited = (lax.ppermute(top, "pipe", across), lax.ppermute(low, "pipe", turned))
            sums = exchange(got, groups)
            mixed = exchange(attend(tick, parts, [sums], waited))
            hops, waited = waited, ()
        operands = [place, own, mixed, out_weight]
        kernel = functools.partial(output_kernel, None)
        if tick < ticks - 1:
            kernel = functools.partial(output_kernel, tick)
            operands.append(fresh)
        result = call(kernel, "project_out", [(tokens, width)], operands, waited)
    top = lax.ppermute(hops[0], "pipe", turned_across)
    low = lax.ppermute(hops[1], "pipe", across)
    evicted = jnp.concatenate([top, low], axis=0)
    return (result[None], evicted[None])


def solution(mesh):
    placed = (
        P("pipe", None, "tp"),
        P(None, None, "tp"),
        P("pipe", "tp"),
        P("pipe", "tp", None),
        P("pipe", None, "tp"),
        P(),
        P("pipe"),
    )
    return jax.shard_map(
        shards,
        mesh=mesh,
        in_specs=placed,
        out_specs=(P("pipe", None, "tp"), P("pipe", None, "tp")),
        check_vma=False,
    )
```

```python
import functools

import jax
import jax.numpy as jnp
from jax import lax
from jax.experimental import pallas as pl
from jax.experimental.pallas import tpu as pltpu
from jax.sharding import PartitionSpec as P

HEAD_DIM = 128
Q_HEADS = 16
Q_COLS = Q_HEADS * HEAD_DIM
KV_COLS = 2 * HEAD_DIM
LONGEST_SEGMENT = 128
NORM_EPS = 1e-05
STEP = 256
F32 = jnp.float32
BF16 = jnp.bfloat16

RANK, INDEX, EVICT = range(3)


def window_blocks(rows):
    return (LONGEST_SEGMENT + rows - 2) // rows + 1


def dot(a, b):
    return jnp.dot(a, b, preferred_element_type=F32)


def project_kernel(pieces, streamed, stashed, place_ref, x_ref, gain_ref, *refs):
    weights, earlier, refs = refs[:pieces], refs[pieces : pieces + stashed], refs[pieces + stashed :]
    out_ref, refs = refs[0], refs[1:]
    if stashed:
        stash_refs, refs = refs[:2], refs[2:]
    made_ref, out_sems, refs = refs[0], refs[1], refs[2:]
    parts, rows, columns = out_ref.shape
    blocks = window_blocks(rows)
    last = columns - 128
    spans = [(start, start + STEP) for start in range(0, Q_COLS + KV_COLS, STEP)]
    if streamed:
        x_held, weight_held, x_sem, weight_sems = refs
        x_copy = pltpu.make_async_copy(x_ref, x_held, x_sem)
        x_copy.start()
        weight_copies = []
        for at, (start, end) in enumerate(spans):
            source, target = weights[0].at[:, start:end], weight_held.at[:, start:end]
            weight_copies.append(pltpu.make_async_copy(source, target, weight_sems.at[at]))
            weight_copies[-1].start()
        x_copy.wait()
        x_ref, weights = x_held, [weight_held]
    elif stashed:
        held_ref, stash_sems = refs
        chosen = x_ref[...]
        for at, earlier_ref in enumerate(earlier):
            chosen = jnp.where(place_ref[EVICT] == at, earlier_ref[...], chosen)
        held_ref[...] = chosen
        middle = chosen.shape[0] // 2
        stash_copies = []
        for at, stash_ref in enumerate(stash_refs):
            source = held_ref.at[at * middle : (at + 1) * middle]
            stash_copies.append(pltpu.make_async_copy(source, stash_ref, stash_sems.at[at]))
            stash_copies[-1].start()
    wide = x_ref[...].astype(F32)
    scaled = (wide * gain_ref[:1].astype(F32)).astype(BF16)
    squares = jnp.sum(wide * wide, axis=1, keepdims=True)
    high = squares.astype(BF16).astype(F32)
    low = squares - high
    depth = scaled.shape[1] // len(weights)
    out_copies = []
    for at, (start, end) in enumerate(spans):
        if streamed:
            weight_copies[at].wait()
        tile = dot(scaled[:, :depth], weights[0][:, start:end])
        for piece in range(1, len(weights)):
            tile = tile + dot(scaled[:, piece * depth : (piece + 1) * depth], weights[piece][:, start:end])
        tile = tile.astype(BF16)
        if start < Q_COLS:
            made_ref[:, :, start:end] = tile.reshape(parts, rows, STEP)
        else:
            lane = lax.broadcasted_iota(jnp.int32, (rows, 128), 1)
            for j in range(parts):
                sums = jnp.zeros((rows, 128), F32)
                for b in range(blocks):
                    first = max(j - blocks + 1 + b, 0) * rows
                    made_ref[j, :, start + b * KV_COLS : start + (b + 1) * KV_COLS] = tile[first : first + rows]
                    sums = jnp.where(lane == 2 * b, high[first : first + rows], sums)
                    sums = jnp.where(lane == 2 * b + 1, low[first : first + rows], sums)
                made_ref[j, :, last:] = sums.astype(BF16)
            end = columns
        source, target = made_ref.at[:, :, start:end], out_ref.at[:, :, start:end]
        out_copies.append(pltpu.make_async_copy(source, target, out_sems.at[at]))
        out_copies[-1].start()
    for copy in out_copies:
        copy.wait()
    if stashed:
        for copy in stash_copies:
            copy.wait()


def piece_kernel(begin, value_ref, *refs):
    out_ref, sem = refs[-2:]
    copy = pltpu.make_async_copy(value_ref.at[begin : begin + out_ref.shape[0]], out_ref, sem)
    copy.start()
    copy.wait()


def spread_kernel(value_ref, waited_ref, out_ref):
    out_ref[...] = jnp.broadcast_to(value_ref[...], out_ref.shape)


def attend_kernel(row, width, place_ref, segments_ref, got_ref, *refs):
    out_ref = refs[-1]
    parts, rows, _ = got_ref.shape
    tokens = rows * parts
    blocks = window_blocks(rows)
    span = blocks * rows
    before = span - rows

    def total(start, size):
        value = got_ref[0, :, start : start + size].astype(F32)
        for j in range(1, parts):
            value = value + got_ref[j, :, start : start + size].astype(F32)
        return value

    sums = total(Q_COLS + blocks * KV_COLS, 128)
    scales = []
    for b in range(blocks):
        squares = sums[:, 2 * b : 2 * b + 1] + sums[:, 2 * b + 1 : 2 * b + 2]
        scales.append(lax.rsqrt(squares / width + NORM_EPS))
    keys, values = [], []
    for b in range(blocks):
        both = (total(Q_COLS + b * KV_COLS, KV_COLS) * scales[b]).astype(BF16)
        keys.append(both[:, :HEAD_DIM])
        values.append(both[:, HEAD_DIM:])
    keys = jnp.concatenate(keys, axis=0)
    values = jnp.concatenate(values, axis=0)
    queries = []
    for h in range(Q_HEADS):
        queries.append((total(h * HEAD_DIM, HEAD_DIM) * scales[-1]).astype(BF16))
    queries = jnp.concatenate(queries, axis=0)

    first = place_ref[RANK] * rows - before
    segment_row = segments_ref[pl.ds(row(place_ref[INDEX]), 1), :]
    segment_row = pltpu.roll(segment_row, lax.rem(tokens - first, tokens), 1)
    segment_rows = jnp.broadcast_to(segment_row, (rows, tokens))
    column = lax.broadcasted_iota(jnp.int32, (rows, tokens), 1)
    own = lax.broadcasted_iota(jnp.int32, (rows, tokens), 0) + before
    own_segment = jnp.sum(jnp.where(column == own, segment_rows, 0), axis=1, keepdims=True)
    visible = (segment_rows == own_segment) & (column <= own) & (column + first >= 0)
    visible = visible[:, :span]

    scores = lax.dot_general(
        queries, keys, (((1,), (1,)), ((), ())), preferred_element_type=F32
    ) * HEAD_DIM ** (-0.5)
    scores = scores.reshape(Q_HEADS, rows, span)
    scores = jnp.where(visible[None], scores, F32(-1e30))
    highest = jnp.max(scores, axis=-1, keepdims=True)
    exponentials = jnp.where(visible[None], jnp.exp(scores - highest), F32(0.0))
    totals = jnp.sum(exponentials, axis=-1, keepdims=True)
    attention = (exponentials / totals).astype(BF16).reshape(Q_HEADS * rows, span)
    mixed = dot(attention, values).astype(BF16)
    for h in range(Q_HEADS):
        piece = mixed[h * rows : (h + 1) * rows]
        for j in range(parts):
            out_ref[j, :, h * HEAD_DIM : (h + 1) * HEAD_DIM] = piece


def output_kernel(pieces, spare, place_ref, x_ref, mixed_ref, *refs):
    out_ref = refs[-1]
    depth = refs[0].shape[0]
    product = dot(mixed_ref[:, :depth], refs[0][...])
    for piece in range(1, pieces):
        product = product + dot(mixed_ref[:, piece * depth : (piece + 1) * depth], refs[piece][...])
    result = (x_ref[...].astype(F32) + product).astype(BF16)
    if spare is not None:
        index, tick = spare
        result = jnp.where(place_ref[INDEX] == index, refs[pieces][tick], result)
    out_ref[...] = result


VMEM = pl.BlockSpec(memory_space=pltpu.VMEM)
SMEM = pl.BlockSpec(memory_space=pltpu.SMEM)
ANY = pl.BlockSpec(memory_space=pl.ANY)
HBM = pl.BlockSpec(memory_space=pltpu.HBM)
PARAMS = pltpu.CompilerParams(vmem_limit_bytes=24 * 1024 * 1024)
ALONE = pltpu.CompilerParams(vmem_limit_bytes=60 * 1024 * 1024)


def shard(*shape):
    return jax.ShapeDtypeStruct(shape, BF16)


def project(place, current, gain, weights, parts, streamed=False, earlier=()):
    tokens, width = current.shape
    rows = tokens // parts
    columns = Q_COLS + window_blocks(rows) * KV_COLS + 128
    tiles = (Q_COLS + KV_COLS) // STEP
    outs = [shard(parts, rows, columns)]
    scratch = [pltpu.VMEM((parts, rows, columns), BF16), pltpu.SemaphoreType.DMA((tiles,))]
    if streamed:
        scratch += [pltpu.VMEM(current.shape, BF16), pltpu.VMEM(weights[0].shape, BF16)]
        scratch += [pltpu.SemaphoreType.DMA, pltpu.SemaphoreType.DMA((tiles,))]
    if earlier:
        outs += [shard(tokens // 2, width)] * 2
        scratch += [pltpu.VMEM(current.shape, BF16), pltpu.SemaphoreType.DMA((2,))]
    space = HBM if streamed else VMEM
    return pl.pallas_call(
        functools.partial(project_kernel, len(weights), streamed, len(earlier)),
        out_shape=outs,
        in_specs=[SMEM, space, VMEM] + [space] * len(weights) + [VMEM] * len(earlier),
        out_specs=[ANY] * len(outs),
        scratch_shapes=scratch,
        compiler_params=ALONE if streamed else PARAMS,
        name="project",
    )(place, current, gain, *weights, *earlier)


def halves(value, waited):
    depth = value.shape[0] // 2
    return [
        pl.pallas_call(
            functools.partial(piece_kernel, begin),
            out_shape=shard(depth, *value.shape[1:]),
            in_specs=[ANY] * (1 + len(waited)),
            out_specs=ANY,
            scratch_shapes=[pltpu.SemaphoreType.DMA],
            compiler_params=PARAMS,
            name="piece",
        )(value, *waited)
        for begin in (0, depth)
    ]


def attend(place, segments, got, row, width, waited):
    parts, rows, _ = got.shape
    return pl.pallas_call(
        functools.partial(attend_kernel, row, width),
        out_shape=shard(parts, rows, Q_COLS),
        in_specs=[SMEM, VMEM, VMEM] + [ANY] * len(waited),
        out_specs=VMEM,
        compiler_params=PARAMS,
        name="attend",
    )(place, segments, got, *waited)


def project_out(place, current, mixed, weights, fresh, spare, waited):
    operands = [current, mixed.reshape(current.shape[0], Q_COLS), *weights]
    if spare is not None:
        operands.append(fresh)
    return pl.pallas_call(
        functools.partial(output_kernel, len(weights), spare),
        out_shape=shard(*current.shape),
        in_specs=[SMEM] + [VMEM] * len(operands) + [ANY] * len(waited),
        out_specs=VMEM,
        compiler_params=PARAMS,
        name="project_out",
    )(place, *operands, *waited)


def shards(carried, fresh, gains, qkv_weight, out_weight, segments, evict_tick):
    index = lax.axis_index("pipe")
    sections = lax.axis_size("pipe")
    parts = lax.axis_size("tp")
    width = carried.shape[2] * parts
    qkv_weight, out_weight = qkv_weight[0], out_weight[0]
    place = jnp.stack([lax.axis_index("tp"), index, evict_tick[0]])
    half = sections // 2
    across = [(i, i + half) for i in range(half)]
    turned = [(i, half - 1 - i) for i in range(half)]
    turned_across = [(half + i, sections - 1 - i) for i in range(half)]

    def move(value, by):
        return lax.ppermute(value, "pipe", [(i, (i + by) % sections) for i in range(sections)])

    def exchange(value):
        return lax.all_to_all(value, "tp", split_axis=0, concat_axis=0, tiled=True)

    start = carried[0]
    partial_proj = project(place, start, gains, [qkv_weight], parts, streamed=True)[0]
    sums = exchange(partial_proj)
    next_gains = pl.pallas_call(
        spread_kernel,
        out_shape=shard(16, gains.shape[1]),
        in_specs=[VMEM, ANY],
        out_specs=VMEM,
        compiler_params=PARAMS,
        name="spread",
    )(gains, partial_proj)
    next_gains = move(next_gains, -1)
    next_qkv = [move(piece, -1) for piece in halves(qkv_weight, (partial_proj,))]
    mixed = attend(place, segments, sums, lambda at: at + 2, width, (next_gains, next_qkv[0]))
    next_out = [move(piece, -1) for piece in halves(out_weight, (mixed,))]
    mixed = exchange(mixed)
    spare = (sections - 1, 0)
    result = project_out(place, start, mixed, [out_weight], fresh, spare, (next_qkv[1],))

    current = result
    sums = exchange(project(place, current, next_gains, next_qkv, parts)[0])
    moved = move(current, 1)
    row = lambda at: lax.rem(at + 1, sections) + 1
    mixed = exchange(attend(place, segments, sums, row, width, (next_out[0],)))
    spare = (sections - 2, 1)
    result = project_out(place, current, mixed, next_out, fresh, spare, (moved,))

    current = move(result, 2)
    got, *stash = project(place, current, gains, [qkv_weight], parts, earlier=(start, moved))
    sums = exchange(got)
    top = lax.ppermute(stash[0], "pipe", across)
    low = lax.ppermute(stash[1], "pipe", turned)
    mixed = exchange(attend(place, segments, sums, lambda at: at, width, (top, low)))
    top = lax.ppermute(top, "pipe", turned_across)
    low = lax.ppermute(low, "pipe", across)
    result = project_out(place, current, mixed, [out_weight], None, None, ())
    evicted = jnp.concatenate([top, low], axis=0)
    return (result[None], evicted[None])


def solution(mesh):
    placed = (
        P("pipe", None, "tp"),
        P(None, None, "tp"),
        P("pipe", "tp"),
        P("pipe", "tp", None),
        P("pipe", None, "tp"),
        P(),
        P("pipe"),
    )
    return jax.shard_map(
        shards,
        mesh=mesh,
        in_specs=placed,
        out_specs=(P("pipe", None, "tp"), P("pipe", None, "tp")),
        check_vma=False,
    )
```

```python
import functools

import jax
import jax.numpy as jnp
from jax import lax
from jax.experimental import pallas as pl
from jax.experimental.pallas import tpu as pltpu
from jax.sharding import PartitionSpec as P

HEAD_DIM = 128
Q_HEADS = 16
Q_COLS = Q_HEADS * HEAD_DIM
KV_COLS = 2 * HEAD_DIM
LONGEST_SEGMENT = 128
NORM_EPS = 1e-05
F32 = jnp.float32
BF16 = jnp.bfloat16


def window_blocks(rows):
    return (LONGEST_SEGMENT + rows - 2) // rows + 1


FIRST, EVICT = range(2)


def copy_all(sources, targets, sems):
    copies = [pltpu.make_async_copy(a, b, sems.at[at]) for at, (a, b) in enumerate(zip(sources, targets))]
    for copy in copies:
        copy.start()
    return copies


def tick_input(tick, flags_ref, arrived_ref, fresh_ref):
    if tick == 0:
        return arrived_ref[...]
    return jnp.where(flags_ref[FIRST] == 1, fresh_ref[tick - 1], arrived_ref[...])


def project_kernel(tick, stash, flags_ref, fresh_ref, gain_ref, weight_ref, *refs):
    arrived, refs = (refs[: tick + 1], refs[tick + 1 :]) if stash else (refs[:1], refs[1:])
    out_ref, refs = refs[0], refs[1:]
    if stash:
        stash_refs, refs = refs[:2], refs[2:]
    made_ref, out_sems, refs = refs[0], refs[1], refs[2:]
    parts, rows, columns = out_ref.shape
    blocks = window_blocks(rows)
    last = columns - 128
    copies = []
    if tick == 0:
        x_held, weight_held, in_sems = refs
        count = in_sems.shape[0] - 1
        depth = weight_held.shape[0] // count
        spans = [slice(at * depth, (at + 1) * depth) for at in range(count)]
        sources = [arrived[0]] + [weight_ref.at[span] for span in spans]
        targets = [x_held] + [weight_held.at[span] for span in spans]
        for copy in copy_all(sources, targets, in_sems):
            copy.wait()
        arrived, weight_ref = [x_held], weight_held
    current = tick_input(tick, flags_ref, arrived[-1], fresh_ref)
    if stash:
        held_ref, stash_sems = refs
        chosen = current
        for at in range(tick):
            chosen = jnp.where(flags_ref[EVICT] == at, tick_input(at, flags_ref, arrived[at], fresh_ref), chosen)
        held_ref[...] = chosen
        middle = chosen.shape[0] // 2
        copies += copy_all([held_ref.at[:middle], held_ref.at[middle:]], stash_refs, stash_sems)
    wide = current.astype(F32)
    scaled = (wide * gain_ref[...].astype(F32)).astype(BF16)
    squares = jnp.sum(wide * wide, axis=1, keepdims=True)
    high = squares.astype(BF16).astype(F32)
    low = squares - high
    lane = lax.broadcasted_iota(jnp.int32, (rows, 128), 1)
    step = 256
    for start in range(0, Q_COLS, step):
        tile = jnp.dot(scaled, weight_ref[:, start : start + step], preferred_element_type=F32)
        made_ref[:, :, start : start + step] = tile.astype(BF16).reshape(parts, rows, step)
    tile = jnp.dot(scaled, weight_ref[:, Q_COLS:], preferred_element_type=F32).astype(BF16)
    for j in range(parts):
        sums = jnp.zeros((rows, 128), F32)
        for b in range(blocks):
            at = max(j - blocks + 1 + b, 0) * rows
            start = Q_COLS + b * KV_COLS
            made_ref[j, :, start : start + KV_COLS] = tile[at : at + rows]
            sums = jnp.where(lane == 2 * b, high[at : at + rows], sums)
            sums = jnp.where(lane == 2 * b + 1, low[at : at + rows], sums)
        made_ref[j, :, last:] = sums.astype(BF16)
        copies.append(pltpu.make_async_copy(made_ref.at[j], out_ref.at[j], out_sems.at[j]))
        copies[-1].start()
    for copy in copies:
        copy.wait()


def attend_kernel(parts, width, place_ref, segments_ref, got_ref, *refs):
    out_ref, held_ref, out_sems = refs[-3:]
    rows = got_ref.shape[1]
    tokens = rows * parts
    blocks = window_blocks(rows)
    span = blocks * rows
    before = span - rows
    rank = place_ref[0]
    item = place_ref[1]

    def total(start, size):
        value = got_ref[0, :, start : start + size].astype(F32)
        for j in range(1, parts):
            value = value + got_ref[j, :, start : start + size].astype(F32)
        return value

    last = Q_COLS + blocks * KV_COLS
    sums = total(last, 128)
    scales = []
    for b in range(blocks):
        squares = sums[:, 2 * b : 2 * b + 1] + sums[:, 2 * b + 1 : 2 * b + 2]
        scales.append(lax.rsqrt(squares / width + NORM_EPS))
    keys, values = [], []
    for b in range(blocks):
        both = (total(Q_COLS + b * KV_COLS, KV_COLS) * scales[b]).astype(BF16)
        keys.append(both[:, :HEAD_DIM])
        values.append(both[:, HEAD_DIM:])
    keys = jnp.concatenate(keys, axis=0)
    values = jnp.concatenate(values, axis=0)
    queries = []
    for h in range(Q_HEADS):
        queries.append((total(h * HEAD_DIM, HEAD_DIM) * scales[-1]).astype(BF16))
    queries = jnp.concatenate(queries, axis=0)

    first = rank * rows - before
    segment_row = segments_ref[pl.ds(item, 1), :]
    segment_row = pltpu.roll(segment_row, lax.rem(tokens - first, tokens), 1)
    segment_rows = jnp.broadcast_to(segment_row, (rows, tokens))
    column = lax.broadcasted_iota(jnp.int32, (rows, tokens), 1)
    own = lax.broadcasted_iota(jnp.int32, (rows, tokens), 0) + before
    own_segment = jnp.sum(jnp.where(column == own, segment_rows, 0), axis=1, keepdims=True)
    visible = (segment_rows == own_segment) & (column <= own) & (column + first >= 0)
    visible = visible[:, :span]

    scores = lax.dot_general(
        queries, keys, (((1,), (1,)), ((), ())), preferred_element_type=F32
    ) * HEAD_DIM ** (-0.5)
    scores = scores.reshape(Q_HEADS, rows, span)
    scores = jnp.where(visible[None], scores, F32(-1e30))
    highest = jnp.max(scores, axis=-1, keepdims=True)
    exponentials = jnp.where(visible[None], jnp.exp(scores - highest), F32(0.0))
    totals = jnp.sum(exponentials, axis=-1, keepdims=True)
    attention = (exponentials / totals).astype(BF16).reshape(Q_HEADS * rows, span)
    mixed = jnp.dot(attention, values, preferred_element_type=F32).astype(BF16)
    for h in range(Q_HEADS):
        held_ref[:, h * HEAD_DIM : (h + 1) * HEAD_DIM] = mixed[h * rows : (h + 1) * rows]
    for copy in copy_all([held_ref] * parts, [out_ref.at[j] for j in range(parts)], out_sems):
        copy.wait()


def output_kernel(tick, flags_ref, fresh_ref, arrived_ref, mixed_ref, weight_ref, *refs):
    copies = []
    out_ref = refs[0]
    if len(refs) > 1:
        top_ref, low_ref, out_ref, evicted_ref, sems = refs
        middle = top_ref.shape[0]
        copies = copy_all([top_ref, low_ref], [evicted_ref.at[:middle], evicted_ref.at[middle:]], sems)
    current = tick_input(tick, flags_ref, arrived_ref, fresh_ref)
    product = jnp.dot(mixed_ref[...], weight_ref[...], preferred_element_type=F32)
    out_ref[...] = (current.astype(F32) + product).astype(BF16)
    for copy in copies:
        copy.wait()


VMEM = pl.BlockSpec(memory_space=pltpu.VMEM)
SMEM = pl.BlockSpec(memory_space=pltpu.SMEM)
ANY = pl.BlockSpec(memory_space=pl.ANY)
HBM = pl.BlockSpec(memory_space=pltpu.HBM)
PARAMS = pltpu.CompilerParams(vmem_limit_bytes=24 * 1024 * 1024)
ALONE = pltpu.CompilerParams(vmem_limit_bytes=60 * 1024 * 1024)
WEIGHT_COPIES = 4


def shard(shape):
    return jax.ShapeDtypeStruct(shape, BF16)


def exchange(value):
    return lax.all_to_all(value, "tp", split_axis=0, concat_axis=0, tiled=True)


def attend(place, segments, got, width, waited=()):
    parts, rows, _ = got.shape
    return pl.pallas_call(
        functools.partial(attend_kernel, parts, width),
        out_shape=shard((parts, rows, Q_COLS)),
        in_specs=[SMEM, VMEM, VMEM] + [ANY] * len(waited),
        out_specs=ANY,
        scratch_shapes=[pltpu.VMEM((rows, Q_COLS), BF16), pltpu.SemaphoreType.DMA((parts,))],
        compiler_params=PARAMS,
        name="attend",
    )(place, segments, got, *waited)


def project(tick, stash, flags, fresh, gains, weight, arrived, parts):
    tokens, width = arrived[0].shape
    rows = tokens // parts
    columns = Q_COLS + window_blocks(rows) * KV_COLS + 128
    outs = [shard((parts, rows, columns))]
    scratch = [pltpu.VMEM((parts, rows, columns), BF16), pltpu.SemaphoreType.DMA((parts,))]
    if tick == 0:
        scratch += [pltpu.VMEM((tokens, width), BF16), pltpu.VMEM(weight.shape, BF16)]
        scratch += [pltpu.SemaphoreType.DMA((1 + WEIGHT_COPIES,))]
    if stash:
        outs += [shard((tokens // 2, width))] * 2
        scratch += [pltpu.VMEM((tokens, width), BF16), pltpu.SemaphoreType.DMA((2,))]
    space = HBM if tick == 0 else VMEM
    return pl.pallas_call(
        functools.partial(project_kernel, tick, stash),
        out_shape=outs,
        in_specs=[SMEM, ANY if tick == 0 else VMEM, VMEM, space] + [space] * len(arrived),
        out_specs=[ANY] * len(outs),
        scratch_shapes=scratch,
        compiler_params=ALONE if tick == 0 else PARAMS,
        name="project",
    )(flags, fresh, gains, weight, *arrived)


def project_out(tick, flags, fresh, arrived, mixed, weight, stash=()):
    outs, out_specs, scratch = [shard(arrived.shape)], [VMEM], []
    if stash:
        outs.append(shard(arrived.shape))
        out_specs.append(ANY)
        scratch.append(pltpu.SemaphoreType.DMA((2,)))
    return pl.pallas_call(
        functools.partial(output_kernel, tick),
        out_shape=outs,
        in_specs=[SMEM, ANY if tick == 0 else VMEM] + [VMEM] * 3 + [ANY] * len(stash),
        out_specs=out_specs,
        scratch_shapes=scratch,
        compiler_params=PARAMS,
        name="project_out",
    )(flags, fresh, arrived, mixed.reshape(arrived.shape[0], Q_COLS), weight, *stash)


def shards(carried, fresh, gains, qkv_weight, out_weight, segments, evict_tick):
    section = lax.axis_index("pipe")
    rank = lax.axis_index("tp")
    sections = lax.axis_size("pipe")
    parts = lax.axis_size("tp")
    ticks = fresh.shape[0] + 1
    width = carried.shape[2] * parts
    qkv_weight, out_weight = qkv_weight[0], out_weight[0]
    flags = jnp.stack([(section == 0).astype(jnp.int32), evict_tick[0]])
    following = [(i, i + 1) for i in range(sections - 1)]
    half = sections // 2
    across = [(i, i + half) for i in range(half)]
    turned = [(i, half - 1 - i) for i in range(half)]
    turned_across = [(half + i, sections - 1 - i) for i in range(half)]
    arrived = [carried[0]]
    for tick in range(ticks):
        stash = tick == ticks - 1
        if tick > 0:
            arrived.append(lax.ppermute(result[0], "pipe", following))
        sources = arrived if stash else arrived[-1:]
        got = project(tick, stash, flags, fresh, gains, qkv_weight, sources, parts)
        sums = exchange(got[0])
        place = jnp.stack([rank, section - tick + ticks - 1]).astype(jnp.int32)
        waited = ()
        if stash:
            waited = (lax.ppermute(got[1], "pipe", across), lax.ppermute(got[2], "pipe", turned))
        mixed = exchange(attend(place, segments, sums, width, waited))
        landed = ()
        if stash:
            landed = (lax.ppermute(waited[0], "pipe", turned_across), lax.ppermute(waited[1], "pipe", across))
        result = project_out(tick, flags, fresh, arrived[-1], mixed, out_weight, landed)
    return (result[0][None], result[1][None])


def solution(mesh):
    placed = (
        P("pipe", None, "tp"),
        P(None, None, "tp"),
        P("pipe", "tp"),
        P("pipe", "tp", None),
        P("pipe", None, "tp"),
        P(),
        P("pipe"),
    )
    return jax.shard_map(
        shards,
        mesh=mesh,
        in_specs=placed,
        out_specs=(P("pipe", None, "tp"), P("pipe", None, "tp")),
        check_vma=False,
    )
```

```python
import functools

import jax
import jax.numpy as jnp
from jax import lax
from jax.experimental import pallas as pl
from jax.experimental.pallas import tpu as pltpu
from jax.sharding import PartitionSpec as P

HEAD_DIM = 128
Q_HEADS = 16
Q_COLS = Q_HEADS * HEAD_DIM
KV_COLS = 2 * HEAD_DIM
LONGEST_SEGMENT = 128
NORM_EPS = 1e-05
F32 = jnp.float32
BF16 = jnp.bfloat16


def window_blocks(rows):
    return (LONGEST_SEGMENT + rows - 2) // rows + 1


def project_rows(parts, wide, scaled, weight_ref, out_ref):
    rows = wide.shape[0] // parts
    blocks = window_blocks(rows)
    squares = jnp.sum(wide * wide, axis=1, keepdims=True)
    high = squares.astype(BF16).astype(F32)
    low = squares - high
    lane = lax.broadcasted_iota(jnp.int32, (rows, 128), 1)
    step = 256
    for start in range(0, Q_COLS, step):
        tile = jnp.dot(scaled, weight_ref[:, start : start + step], preferred_element_type=F32)
        out_ref[:, :, start : start + step] = tile.astype(BF16).reshape(parts, rows, step)
    tile = jnp.dot(scaled, weight_ref[:, Q_COLS:], preferred_element_type=F32).astype(BF16)
    last = Q_COLS + blocks * KV_COLS
    for j in range(parts):
        sums = jnp.zeros((rows, 128), F32)
        for b in range(blocks):
            at = max(j - blocks + 1 + b, 0) * rows
            start = Q_COLS + b * KV_COLS
            out_ref[j, :, start : start + KV_COLS] = tile[at : at + rows]
            sums = jnp.where(lane == 2 * b, high[at : at + rows], sums)
            sums = jnp.where(lane == 2 * b + 1, low[at : at + rows], sums)
        out_ref[j, :, last:] = sums.astype(BF16)


FIRST, EVICT, RANK, SECTION = range(4)


def project_kernel(parts, tick, stash, flags_ref, *refs):
    earlier, refs = (refs[:tick], refs[tick:]) if stash else ((), refs)
    if tick > 0:
        arrived_ref, fresh_ref, gain_ref, weight_ref, out_ref, current_ref = refs[:6]
        current = jnp.where(flags_ref[FIRST] == 1, fresh_ref[tick - 1], arrived_ref[...])
        current_ref[...] = current
    else:
        arrived_ref, gain_ref, weight_ref, out_ref = refs
        current = arrived_ref[...]
    if earlier:
        chosen = current
        for at, earlier_ref in enumerate(earlier):
            chosen = jnp.where(flags_ref[EVICT] == at, earlier_ref[...], chosen)
        half = chosen.shape[0] // 2
        refs[6][...] = chosen[:half]
        refs[7][...] = chosen[half:]
    wide = current.astype(F32)
    scaled = (wide * gain_ref[...].astype(F32)).astype(BF16)
    project_rows(parts, wide, scaled, weight_ref, out_ref)


def attend_kernel(parts, width, back, flags_ref, segments_ref, got_ref, *refs):
    out_ref = refs[-1]
    rows = got_ref.shape[1]
    tokens = rows * parts
    blocks = window_blocks(rows)
    span = blocks * rows
    before = span - rows
    rank = flags_ref[RANK]
    item = flags_ref[SECTION] + back

    def total(start, size):
        value = got_ref[0, :, start : start + size].astype(F32)
        for j in range(1, parts):
            value = value + got_ref[j, :, start : start + size].astype(F32)
        return value

    last = Q_COLS + blocks * KV_COLS
    sums = total(last, 128)
    scales = []
    for b in range(blocks):
        squares = sums[:, 2 * b : 2 * b + 1] + sums[:, 2 * b + 1 : 2 * b + 2]
        scales.append(lax.rsqrt(squares / width + NORM_EPS))
    keys, values = [], []
    for b in range(blocks):
        both = (total(Q_COLS + b * KV_COLS, KV_COLS) * scales[b]).astype(BF16)
        keys.append(both[:, :HEAD_DIM])
        values.append(both[:, HEAD_DIM:])
    keys = jnp.concatenate(keys, axis=0)
    values = jnp.concatenate(values, axis=0)
    queries = []
    for h in range(Q_HEADS):
        queries.append((total(h * HEAD_DIM, HEAD_DIM) * scales[-1]).astype(BF16))
    queries = jnp.concatenate(queries, axis=0)

    first = rank * rows - before
    segment_row = segments_ref[pl.ds(item, 1), :]
    segment_row = pltpu.roll(segment_row, lax.rem(tokens - first, tokens), 1)
    segment_rows = jnp.broadcast_to(segment_row, (rows, tokens))
    column = lax.broadcasted_iota(jnp.int32, (rows, tokens), 1)
    own = lax.broadcasted_iota(jnp.int32, (rows, tokens), 0) + before
    own_segment = jnp.sum(jnp.where(column == own, segment_rows, 0), axis=1, keepdims=True)
    visible = (segment_rows == own_segment) & (column <= own) & (column + first >= 0)
    visible = visible[:, :span]

    scores = lax.dot_general(
        queries, keys, (((1,), (1,)), ((), ())), preferred_element_type=F32
    ) * HEAD_DIM ** (-0.5)
    scores = scores.reshape(Q_HEADS, rows, span)
    scores = jnp.where(visible[None], scores, F32(-1e30))
    highest = jnp.max(scores, axis=-1, keepdims=True)
    exponentials = jnp.where(visible[None], jnp.exp(scores - highest), F32(0.0))
    totals = jnp.sum(exponentials, axis=-1, keepdims=True)
    attention = (exponentials / totals).astype(BF16).reshape(Q_HEADS * rows, span)
    mixed = jnp.dot(attention, values, preferred_element_type=F32).astype(BF16)
    for h in range(Q_HEADS):
        piece = mixed[h * rows : (h + 1) * rows]
        for j in range(parts):
            out_ref[j, :, h * HEAD_DIM : (h + 1) * HEAD_DIM] = piece


def output_kernel(x_ref, mixed_ref, weight_ref, out_ref):
    product = jnp.dot(mixed_ref[...], weight_ref[...], preferred_element_type=F32)
    out_ref[...] = (x_ref[...].astype(F32) + product).astype(BF16)


VMEM = pl.BlockSpec(memory_space=pltpu.VMEM)
SMEM = pl.BlockSpec(memory_space=pltpu.SMEM)
ANY = pl.BlockSpec(memory_space=pl.ANY)
PARAMS = pltpu.CompilerParams(vmem_limit_bytes=24 * 1024 * 1024)


def shard(shape):
    return jax.ShapeDtypeStruct(shape, BF16)


def exchange(value):
    return lax.all_to_all(value, "tp", split_axis=0, concat_axis=0, tiled=True)


def attend(flags, segments, got, width, back, waited=()):
    parts, rows, _ = got.shape
    return pl.pallas_call(
        functools.partial(attend_kernel, parts, width, back),
        out_shape=shard((parts, rows, Q_COLS)),
        in_specs=[SMEM, VMEM, VMEM] + [ANY] * len(waited),
        out_specs=VMEM,
        compiler_params=PARAMS,
        name="attend",
    )(flags, segments, got, *waited)


def project_out(current, mixed, out_weight):
    return pl.pallas_call(
        output_kernel,
        out_shape=shard(current.shape),
        in_specs=[VMEM] * 3,
        out_specs=VMEM,
        compiler_params=PARAMS,
        name="project_out",
    )(current, mixed.reshape(current.shape[0], Q_COLS), out_weight)


def shards(carried, fresh, gains, qkv_weight, out_weight, segments, evict_tick):
    section = lax.axis_index("pipe")
    rank = lax.axis_index("tp")
    sections = lax.axis_size("pipe")
    parts = lax.axis_size("tp")
    ticks = fresh.shape[0] + 1
    tokens, width = carried.shape[1:]
    rows = tokens // parts
    columns = Q_COLS + window_blocks(rows) * KV_COLS + 128
    flags = jnp.stack([(section == 0).astype(jnp.int32), evict_tick[0], rank, section])
    following = [(i, i + 1) for i in range(sections - 1)]
    half = sections // 2
    across = [(i, i + half) for i in range(half)]
    turned = [(i, half - 1 - i) for i in range(half)]
    turned_across = [(half + i, sections - 1 - i) for i in range(half)]
    inputs = [carried[0]]
    for tick in range(ticks):
        outs = [shard((parts, rows, columns))]
        operands = [flags, inputs[0], gains, qkv_weight[0]]
        specs = [SMEM, VMEM, VMEM, VMEM]
        if tick > 0:
            arrived = lax.ppermute(result, "pipe", following)
            operands = [flags, arrived, fresh, gains, qkv_weight[0]]
            specs = [SMEM, VMEM, VMEM, VMEM, VMEM]
            outs.append(shard((tokens, width)))
        if tick == ticks - 1:
            operands[1:1] = inputs
            specs[1:1] = [VMEM] * tick
            outs += [shard((tokens // 2, width))] * 2
        got = pl.pallas_call(
            functools.partial(project_kernel, parts, tick, tick == ticks - 1),
            out_shape=outs,
            in_specs=specs,
            out_specs=[VMEM] * len(outs),
            compiler_params=PARAMS,
            name="project",
        )(*operands)
        partial_proj = got[0]
        if tick > 0:
            inputs.append(got[1])
        sums = exchange(partial_proj)
        waited = ()
        if tick == ticks - 1:
            waited = (lax.ppermute(got[2], "pipe", across), lax.ppermute(got[3], "pipe", turned))
        mixed = exchange(attend(flags, segments, sums, width * parts, ticks - 1 - tick, waited))
        result = project_out(inputs[tick], mixed, out_weight[0])
    top = lax.ppermute(waited[0], "pipe", turned_across)
    low = lax.ppermute(waited[1], "pipe", across)
    evicted = jnp.concatenate([top, low], axis=0)
    return (result[None], evicted[None])


def solution(mesh):
    placed = (
        P("pipe", None, "tp"),
        P(None, None, "tp"),
        P("pipe", "tp"),
        P("pipe", "tp", None),
        P("pipe", None, "tp"),
        P(),
        P("pipe"),
    )
    return jax.shard_map(
        shards,
        mesh=mesh,
        in_specs=placed,
        out_specs=(P("pipe", None, "tp"), P("pipe", None, "tp")),
        check_vma=False,
    )
```

```python
import functools

import jax
import jax.numpy as jnp
from jax import lax
from jax.experimental import pallas as pl
from jax.experimental.pallas import tpu as pltpu
from jax.sharding import PartitionSpec as P

HEAD_DIM = 128
Q_HEADS = 16
Q_COLS = Q_HEADS * HEAD_DIM
KV_COLS = 2 * HEAD_DIM
LONGEST_SEGMENT = 128
NORM_EPS = 1e-05
F32 = jnp.float32
BF16 = jnp.bfloat16


def window_blocks(rows):
    return (LONGEST_SEGMENT + rows - 2) // rows + 1


def project_rows(parts, wide, scaled, weight_ref, out_ref):
    tokens = wide.shape[0]
    rows = tokens // parts
    blocks = window_blocks(rows)
    ones = jnp.ones((8, wide.shape[1]), BF16)
    squares = lax.dot_general(
        ones, (wide * wide).astype(BF16), (((1,), (1,)), ((), ())), preferred_element_type=F32
    )[:1]
    top = lax.broadcasted_iota(jnp.int32, (rows, KV_COLS), 0) == 0
    step = 256
    for start in range(0, Q_COLS, step):
        tile = jnp.dot(scaled, weight_ref[:, start : start + step], preferred_element_type=F32)
        out_ref[:, :, start : start + step] = tile.astype(BF16).reshape(parts, rows, step)
    tile = jnp.dot(scaled, weight_ref[:, Q_COLS:], preferred_element_type=F32)
    for j in range(parts):
        first = (j + 1 - blocks) * rows
        sums = pltpu.roll(squares, -first % tokens, 1) if first % tokens else squares
        for b in range(blocks):
            at = max(first + b * rows, 0)
            start = Q_COLS + b * KV_COLS
            piece = tile[at : at + rows]
            if b == 0:
                piece = jnp.where(top, jnp.broadcast_to(sums[:, :KV_COLS], piece.shape), piece)
            out_ref[j, :, start : start + KV_COLS] = piece.astype(BF16)


FIRST, EVICT, RANK, SECTION = range(4)


def project_kernel(parts, tick, stash, flags_ref, *refs):
    earlier, refs = (refs[:tick], refs[tick:]) if stash else ((), refs)
    if tick > 0:
        arrived_ref, fresh_ref, gain_ref, weight_ref, out_ref, current_ref = refs[:6]
        current = jnp.where(flags_ref[FIRST] == 1, fresh_ref[tick - 1], arrived_ref[...])
        current_ref[...] = current
    else:
        arrived_ref, gain_ref, weight_ref, out_ref = refs
        current = arrived_ref[...]
    if earlier:
        chosen = current
        for at, earlier_ref in enumerate(earlier):
            chosen = jnp.where(flags_ref[EVICT] == at, earlier_ref[...], chosen)
        half = chosen.shape[0] // 2
        refs[6][...] = chosen[:half]
        refs[7][...] = chosen[half:]
    wide = current.astype(F32)
    scaled = (wide * gain_ref[...].astype(F32)).astype(BF16)
    project_rows(parts, wide, scaled, weight_ref, out_ref)


def attend_kernel(parts, width, back, flags_ref, segments_ref, got_ref, *refs):
    out_ref = refs[-1]
    rows = got_ref.shape[1]
    tokens = rows * parts
    blocks = window_blocks(rows)
    span = blocks * rows
    before = span - rows
    rank = flags_ref[RANK]
    item = flags_ref[SECTION] + back

    def total(start, size):
        value = got_ref[0, :, start : start + size].astype(F32)
        for j in range(1, parts):
            value = value + got_ref[j, :, start : start + size].astype(F32)
        return value

    column = lax.broadcasted_iota(jnp.int32, (rows, tokens), 1)
    row = lax.broadcasted_iota(jnp.int32, (rows, tokens), 0)
    windows = [total(Q_COLS + b * KV_COLS, KV_COLS) for b in range(blocks)]
    sums = jnp.broadcast_to(windows[0][:1], (rows, KV_COLS))
    scales, keys, values = [], [], []
    for b in range(blocks):
        squares = jnp.sum(jnp.where(column == row + b * rows, sums, F32(0.0)), axis=1, keepdims=True)
        scales.append(lax.rsqrt(squares / width + NORM_EPS))
        both = (windows[b] * scales[b]).astype(BF16)
        keys.append(both[:, :HEAD_DIM])
        values.append(both[:, HEAD_DIM:])
    keys = jnp.concatenate(keys, axis=0)
    values = jnp.concatenate(values, axis=0)
    queries = []
    for h in range(Q_HEADS):
        queries.append((total(h * HEAD_DIM, HEAD_DIM) * scales[-1]).astype(BF16))
    queries = jnp.concatenate(queries, axis=0)

    first = rank * rows - before
    segment_row = segments_ref[pl.ds(item, 1), :]
    segment_row = pltpu.roll(segment_row, lax.rem(tokens - first, tokens), 1)
    segment_rows = jnp.broadcast_to(segment_row, (rows, tokens))
    own = row + before
    own_segment = jnp.sum(jnp.where(column == own, segment_rows, 0), axis=1, keepdims=True)
    visible = (segment_rows == own_segment) & (column <= own) & (column + first >= 0) & (column >= 1)
    visible = visible[:, :span]

    scores = lax.dot_general(
        queries, keys, (((1,), (1,)), ((), ())), preferred_element_type=F32
    ) * HEAD_DIM ** (-0.5)
    scores = scores.reshape(Q_HEADS, rows, span)
    scores = jnp.where(visible[None], scores, F32(-1e30))
    highest = jnp.max(scores, axis=-1, keepdims=True)
    exponentials = jnp.where(visible[None], jnp.exp(scores - highest), F32(0.0))
    totals = jnp.sum(exponentials, axis=-1, keepdims=True)
    attention = (exponentials / totals).astype(BF16).reshape(Q_HEADS * rows, span)
    mixed = jnp.dot(attention, values, preferred_element_type=F32).astype(BF16)
    for h in range(Q_HEADS):
        piece = mixed[h * rows : (h + 1) * rows]
        for j in range(parts):
            out_ref[j, :, h * HEAD_DIM : (h + 1) * HEAD_DIM] = piece


def output_kernel(x_ref, mixed_ref, weight_ref, out_ref):
    product = jnp.dot(mixed_ref[...], weight_ref[...], preferred_element_type=F32)
    out_ref[...] = (x_ref[...].astype(F32) + product).astype(BF16)


VMEM = pl.BlockSpec(memory_space=pltpu.VMEM)
SMEM = pl.BlockSpec(memory_space=pltpu.SMEM)
ANY = pl.BlockSpec(memory_space=pl.ANY)
PARAMS = pltpu.CompilerParams(vmem_limit_bytes=24 * 1024 * 1024)


def shard(shape):
    return jax.ShapeDtypeStruct(shape, BF16)


def exchange(value):
    return lax.all_to_all(value, "tp", split_axis=0, concat_axis=0, tiled=True)


def attend(flags, segments, got, width, back, waited=()):
    parts, rows, _ = got.shape
    return pl.pallas_call(
        functools.partial(attend_kernel, parts, width, back),
        out_shape=shard((parts, rows, Q_COLS)),
        in_specs=[SMEM, VMEM, VMEM] + [ANY] * len(waited),
        out_specs=VMEM,
        compiler_params=PARAMS,
        name="attend",
    )(flags, segments, got, *waited)


def project_out(current, mixed, out_weight):
    return pl.pallas_call(
        output_kernel,
        out_shape=shard(current.shape),
        in_specs=[VMEM] * 3,
        out_specs=VMEM,
        compiler_params=PARAMS,
        name="project_out",
    )(current, mixed.reshape(current.shape[0], Q_COLS), out_weight)


def shards(carried, fresh, gains, qkv_weight, out_weight, segments, evict_tick):
    section = lax.axis_index("pipe")
    rank = lax.axis_index("tp")
    sections = lax.axis_size("pipe")
    parts = lax.axis_size("tp")
    ticks = fresh.shape[0] + 1
    tokens, width = carried.shape[1:]
    rows = tokens // parts
    columns = Q_COLS + window_blocks(rows) * KV_COLS
    flags = jnp.stack([(section == 0).astype(jnp.int32), evict_tick[0], rank, section])
    following = [(i, i + 1) for i in range(sections - 1)]
    half = sections // 2
    across = [(i, i + half) for i in range(half)]
    turned = [(i, half - 1 - i) for i in range(half)]
    turned_across = [(half + i, sections - 1 - i) for i in range(half)]
    inputs = [carried[0]]
    for tick in range(ticks):
        outs = [shard((parts, rows, columns))]
        operands = [flags, inputs[0], gains, qkv_weight[0]]
        specs = [SMEM, VMEM, VMEM, VMEM]
        if tick > 0:
            arrived = lax.ppermute(result, "pipe", following)
            operands = [flags, arrived, fresh, gains, qkv_weight[0]]
            specs = [SMEM, VMEM, VMEM, VMEM, VMEM]
            outs.append(shard((tokens, width)))
        if tick == ticks - 1:
            operands[1:1] = inputs
            specs[1:1] = [VMEM] * tick
            outs += [shard((tokens // 2, width))] * 2
        got = pl.pallas_call(
            functools.partial(project_kernel, parts, tick, tick == ticks - 1),
            out_shape=outs,
            in_specs=specs,
            out_specs=[VMEM] * len(outs),
            compiler_params=PARAMS,
            name="project",
        )(*operands)
        partial_proj = got[0]
        if tick > 0:
            inputs.append(got[1])
        sums = exchange(partial_proj)
        waited = ()
        if tick == ticks - 1:
            waited = (lax.ppermute(got[2], "pipe", across), lax.ppermute(got[3], "pipe", turned))
        mixed = exchange(attend(flags, segments, sums, width * parts, ticks - 1 - tick, waited))
        result = project_out(inputs[tick], mixed, out_weight[0])
    top = lax.ppermute(waited[0], "pipe", turned_across)
    low = lax.ppermute(waited[1], "pipe", across)
    evicted = jnp.concatenate([top, low], axis=0)
    return (result[None], evicted[None])


def solution(mesh):
    placed = (
        P("pipe", None, "tp"),
        P(None, None, "tp"),
        P("pipe", "tp"),
        P("pipe", "tp", None),
        P("pipe", None, "tp"),
        P(),
        P("pipe"),
    )
    return jax.shard_map(
        shards,
        mesh=mesh,
        in_specs=placed,
        out_specs=(P("pipe", None, "tp"), P("pipe", None, "tp")),
        check_vma=False,
    )
```

```python
import functools

import jax
import jax.numpy as jnp
from jax import lax
from jax.experimental import pallas as pl
from jax.experimental.pallas import tpu as pltpu
from jax.sharding import PartitionSpec as P

HEAD_DIM = 128
Q_HEADS = 16
Q_COLS = Q_HEADS * HEAD_DIM
KV_COLS = 2 * HEAD_DIM
LONGEST_SEGMENT = 128
NORM_EPS = 1e-05
F32 = jnp.float32
BF16 = jnp.bfloat16


def window_blocks(rows):
    return (LONGEST_SEGMENT + rows - 2) // rows + 1


def project_rows(parts, wide, scaled, weight_ref, out_ref):
    tokens = wide.shape[0]
    rows = tokens // parts
    blocks = window_blocks(rows)
    ones = jnp.ones((8, wide.shape[1]), BF16)
    squares = lax.dot_general(
        ones, (wide * wide).astype(BF16), (((1,), (1,)), ((), ())), preferred_element_type=F32
    )[:1]
    top = lax.broadcasted_iota(jnp.int32, (rows, KV_COLS), 0) == 0
    step = 256
    for start in range(0, Q_COLS, step):
        tile = jnp.dot(scaled, weight_ref[:, start : start + step], preferred_element_type=F32)
        out_ref[:, :, start : start + step] = tile.astype(BF16).reshape(parts, rows, step)
    tile = jnp.dot(scaled, weight_ref[:, Q_COLS:], preferred_element_type=F32)
    for j in range(parts):
        first = (j + 1 - blocks) * rows
        sums = pltpu.roll(squares, -first % tokens, 1) if first % tokens else squares
        for b in range(blocks):
            at = max(first + b * rows, 0)
            start = Q_COLS + b * KV_COLS
            piece = tile[at : at + rows]
            if b == 0:
                piece = jnp.where(top, jnp.broadcast_to(sums[:, :KV_COLS], piece.shape), piece)
            out_ref[j, :, start : start + KV_COLS] = piece.astype(BF16)


def project_kernel(parts, tick, stash, *refs):
    earlier = ()
    if stash:
        evict_ref, earlier, refs = refs[0], refs[1 : tick + 1], refs[tick + 1 :]
    if tick > 0:
        arrived_ref, fresh_ref, gain_ref, weight_ref, out_ref, current_ref = refs[:6]
        current = jnp.where(lax.axis_index("pipe") == 0, fresh_ref[tick - 1], arrived_ref[...])
        current_ref[...] = current
    else:
        arrived_ref, gain_ref, weight_ref, out_ref = refs
        current = arrived_ref[...]
    if earlier:
        chosen = current
        for at, earlier_ref in enumerate(earlier):
            chosen = jnp.where(evict_ref[0] == at, earlier_ref[...], chosen)
        half = chosen.shape[0] // 2
        refs[6][...] = chosen[:half]
        refs[7][...] = chosen[half:]
    wide = current.astype(F32)
    scaled = (wide * gain_ref[...].astype(F32)).astype(BF16)
    project_rows(parts, wide, scaled, weight_ref, out_ref)


def attend_kernel(parts, width, back, segments_ref, got_ref, *refs):
    out_ref = refs[-1]
    rows = got_ref.shape[1]
    tokens = rows * parts
    blocks = window_blocks(rows)
    span = blocks * rows
    before = span - rows
    rank = lax.axis_index("tp")
    item = lax.axis_index("pipe") + back

    def total(start, size):
        value = got_ref[0, :, start : start + size].astype(F32)
        for j in range(1, parts):
            value = value + got_ref[j, :, start : start + size].astype(F32)
        return value

    column = lax.broadcasted_iota(jnp.int32, (rows, tokens), 1)
    row = lax.broadcasted_iota(jnp.int32, (rows, tokens), 0)
    windows = [total(Q_COLS + b * KV_COLS, KV_COLS) for b in range(blocks)]
    sums = jnp.broadcast_to(windows[0][:1], (rows, KV_COLS))
    scales, keys, values = [], [], []
    for b in range(blocks):
        squares = jnp.sum(jnp.where(column == row + b * rows, sums, F32(0.0)), axis=1, keepdims=True)
        scales.append(lax.rsqrt(squares / width + NORM_EPS))
        both = (windows[b] * scales[b]).astype(BF16)
        keys.append(both[:, :HEAD_DIM])
        values.append(both[:, HEAD_DIM:])
    keys = jnp.concatenate(keys, axis=0)
    values = jnp.concatenate(values, axis=0)
    queries = []
    for h in range(Q_HEADS):
        queries.append((total(h * HEAD_DIM, HEAD_DIM) * scales[-1]).astype(BF16))
    queries = jnp.concatenate(queries, axis=0)

    first = rank * rows - before
    segment_row = segments_ref[pl.ds(item, 1), :]
    segment_row = pltpu.roll(segment_row, lax.rem(tokens - first, tokens), 1)
    segment_rows = jnp.broadcast_to(segment_row, (rows, tokens))
    own = row + before
    own_segment = jnp.sum(jnp.where(column == own, segment_rows, 0), axis=1, keepdims=True)
    visible = (segment_rows == own_segment) & (column <= own) & (column + first >= 0) & (column >= 1)
    visible = visible[:, :span]

    scores = lax.dot_general(
        queries, keys, (((1,), (1,)), ((), ())), preferred_element_type=F32
    ) * HEAD_DIM ** (-0.5)
    scores = scores.reshape(Q_HEADS, rows, span)
    scores = jnp.where(visible[None], scores, F32(-1e30))
    highest = jnp.max(scores, axis=-1, keepdims=True)
    exponentials = jnp.where(visible[None], jnp.exp(scores - highest), F32(0.0))
    totals = jnp.sum(exponentials, axis=-1, keepdims=True)
    attention = (exponentials / totals).astype(BF16).reshape(Q_HEADS * rows, span)
    mixed = jnp.dot(attention, values, preferred_element_type=F32).astype(BF16)
    for h in range(Q_HEADS):
        piece = mixed[h * rows : (h + 1) * rows]
        for j in range(parts):
            out_ref[j, :, h * HEAD_DIM : (h + 1) * HEAD_DIM] = piece


def output_kernel(x_ref, mixed_ref, weight_ref, out_ref):
    product = jnp.dot(mixed_ref[...], weight_ref[...], preferred_element_type=F32)
    out_ref[...] = (x_ref[...].astype(F32) + product).astype(BF16)


VMEM = pl.BlockSpec(memory_space=pltpu.VMEM)
SMEM = pl.BlockSpec(memory_space=pltpu.SMEM)
ANY = pl.BlockSpec(memory_space=pl.ANY)
PARAMS = pltpu.CompilerParams(vmem_limit_bytes=24 * 1024 * 1024)


def shard(shape):
    return jax.ShapeDtypeStruct(shape, BF16)


def exchange(value):
    return lax.all_to_all(value, "tp", split_axis=0, concat_axis=0, tiled=True)


def attend(segments, got, width, back, waited=()):
    parts, rows, _ = got.shape
    return pl.pallas_call(
        functools.partial(attend_kernel, parts, width, back),
        out_shape=shard((parts, rows, Q_COLS)),
        in_specs=[VMEM, VMEM] + [ANY] * len(waited),
        out_specs=VMEM,
        compiler_params=PARAMS,
        name="attend",
    )(segments, got, *waited)


def project_out(current, mixed, out_weight):
    return pl.pallas_call(
        output_kernel,
        out_shape=shard(current.shape),
        in_specs=[VMEM] * 3,
        out_specs=VMEM,
        compiler_params=PARAMS,
        name="project_out",
    )(current, mixed.reshape(current.shape[0], Q_COLS), out_weight)


def shards(carried, fresh, gains, qkv_weight, out_weight, segments, evict_tick):
    sections = lax.axis_size("pipe")
    parts = lax.axis_size("tp")
    ticks = fresh.shape[0] + 1
    tokens, width = carried.shape[1:]
    rows = tokens // parts
    columns = Q_COLS + window_blocks(rows) * KV_COLS
    following = [(i, i + 1) for i in range(sections - 1)]
    half = sections // 2
    across = [(i, i + half) for i in range(half)]
    turned = [(i, half - 1 - i) for i in range(half)]
    turned_across = [(half + i, sections - 1 - i) for i in range(half)]
    inputs = [carried[0]]
    for tick in range(ticks):
        outs = [shard((parts, rows, columns))]
        operands = [inputs[0], gains, qkv_weight[0]]
        specs = [VMEM] * 3
        if tick > 0:
            arrived = lax.ppermute(result, "pipe", following)
            operands = [arrived, fresh, gains, qkv_weight[0]]
            specs = [VMEM] * 4
            outs.append(shard((tokens, width)))
        if tick == ticks - 1:
            operands[:0] = [evict_tick, *inputs]
            specs[:0] = [SMEM] + [VMEM] * tick
            outs += [shard((tokens // 2, width))] * 2
        got = pl.pallas_call(
            functools.partial(project_kernel, parts, tick, tick == ticks - 1),
            out_shape=outs,
            in_specs=specs,
            out_specs=[VMEM] * len(outs),
            compiler_params=PARAMS,
            name="project",
        )(*operands)
        partial_proj = got[0]
        if tick > 0:
            inputs.append(got[1])
        sums = exchange(partial_proj)
        waited = ()
        if tick == ticks - 1:
            waited = (lax.ppermute(got[2], "pipe", across), lax.ppermute(got[3], "pipe", turned))
        mixed = exchange(attend(segments, sums, width * parts, ticks - 1 - tick, waited))
        result = project_out(inputs[tick], mixed, out_weight[0])
    top = lax.ppermute(waited[0], "pipe", turned_across)
    low = lax.ppermute(waited[1], "pipe", across)
    evicted = jnp.concatenate([top, low], axis=0)
    return (result[None], evicted[None])


def solution(mesh):
    placed = (
        P("pipe", None, "tp"),
        P(None, None, "tp"),
        P("pipe", "tp"),
        P("pipe", "tp", None),
        P("pipe", None, "tp"),
        P(),
        P("pipe"),
    )
    return jax.shard_map(
        shards,
        mesh=mesh,
        in_specs=placed,
        out_specs=(P("pipe", None, "tp"), P("pipe", None, "tp")),
        check_vma=False,
    )
```

```python
import functools

import jax
import jax.numpy as jnp
from jax import lax
from jax.experimental import pallas as pl
from jax.experimental.pallas import tpu as pltpu
from jax.sharding import PartitionSpec as P

HEAD_DIM = 128
Q_HEADS = 16
Q_COLS = Q_HEADS * HEAD_DIM
KV_COLS = 2 * HEAD_DIM
LONGEST_SEGMENT = 128
NORM_EPS = 1e-05
F32 = jnp.float32
BF16 = jnp.bfloat16


def window_blocks(rows):
    return (LONGEST_SEGMENT + rows - 2) // rows + 1


def project_rows(parts, wide, scaled, weight_ref, out_ref):
    tokens = wide.shape[0]
    rows = tokens // parts
    blocks = window_blocks(rows)
    ones = jnp.ones((8, wide.shape[1]), BF16)
    squares = lax.dot_general(
        ones, (wide * wide).astype(BF16), (((1,), (1,)), ((), ())), preferred_element_type=F32
    )[:1]
    top = lax.broadcasted_iota(jnp.int32, (rows, KV_COLS), 0) == 0
    step = 256
    for start in range(0, Q_COLS, step):
        tile = jnp.dot(scaled, weight_ref[:, start : start + step], preferred_element_type=F32)
        out_ref[:, :, start : start + step] = tile.astype(BF16).reshape(parts, rows, step)
    tile = jnp.dot(scaled, weight_ref[:, Q_COLS:], preferred_element_type=F32)
    for j in range(parts):
        first = (j + 1 - blocks) * rows
        sums = pltpu.roll(squares, -first % tokens, 1) if first % tokens else squares
        for b in range(blocks):
            at = max(first + b * rows, 0)
            start = Q_COLS + b * KV_COLS
            piece = tile[at : at + rows]
            if b == 0:
                piece = jnp.where(top, jnp.broadcast_to(sums[:, :KV_COLS], piece.shape), piece)
            out_ref[j, :, start : start + KV_COLS] = piece.astype(BF16)


def project_kernel(parts, tick, stash, *refs):
    earlier = ()
    if stash:
        evict_ref, earlier, refs = refs[0], refs[1 : tick + 1], refs[tick + 1 :]
    if tick > 0:
        arrived_ref, fresh_ref, gain_ref, weight_ref, out_ref, current_ref = refs[:6]
        current = jnp.where(lax.axis_index("pipe") == 0, fresh_ref[tick - 1], arrived_ref[...])
        current_ref[...] = current
    else:
        arrived_ref, gain_ref, weight_ref, out_ref = refs
        current = arrived_ref[...]
    if earlier:
        chosen = current
        evict = jnp.max(evict_ref[...])
        for at, earlier_ref in enumerate(earlier):
            chosen = jnp.where(evict == at, earlier_ref[...], chosen)
        half = chosen.shape[0] // 2
        refs[6][...] = chosen[:half]
        refs[7][...] = chosen[half:]
    wide = current.astype(F32)
    scaled = (wide * gain_ref[...].astype(F32)).astype(BF16)
    project_rows(parts, wide, scaled, weight_ref, out_ref)


def attend_kernel(parts, width, back, segments_ref, got_ref, *refs):
    out_ref = refs[-1]
    rows = got_ref.shape[1]
    tokens = rows * parts
    blocks = window_blocks(rows)
    span = blocks * rows
    before = span - rows
    rank = lax.axis_index("tp")
    item = lax.axis_index("pipe") + back

    def total(start, size):
        value = got_ref[0, :, start : start + size].astype(F32)
        for j in range(1, parts):
            value = value + got_ref[j, :, start : start + size].astype(F32)
        return value

    column = lax.broadcasted_iota(jnp.int32, (rows, tokens), 1)
    row = lax.broadcasted_iota(jnp.int32, (rows, tokens), 0)
    windows = [total(Q_COLS + b * KV_COLS, KV_COLS) for b in range(blocks)]
    sums = jnp.broadcast_to(windows[0][:1], (rows, KV_COLS))
    scales, keys, values = [], [], []
    for b in range(blocks):
        squares = jnp.sum(jnp.where(column == row + b * rows, sums, F32(0.0)), axis=1, keepdims=True)
        scales.append(lax.rsqrt(squares / width + NORM_EPS))
        both = (windows[b] * scales[b]).astype(BF16)
        keys.append(both[:, :HEAD_DIM])
        values.append(both[:, HEAD_DIM:])
    keys = jnp.concatenate(keys, axis=0)
    values = jnp.concatenate(values, axis=0)
    queries = []
    for h in range(Q_HEADS):
        queries.append((total(h * HEAD_DIM, HEAD_DIM) * scales[-1]).astype(BF16))
    queries = jnp.concatenate(queries, axis=0)

    first = rank * rows - before
    segment_row = segments_ref[pl.ds(item, 1), :]
    segment_row = pltpu.roll(segment_row, lax.rem(tokens - first, tokens), 1)
    segment_rows = jnp.broadcast_to(segment_row, (rows, tokens))
    own = row + before
    own_segment = jnp.sum(jnp.where(column == own, segment_rows, 0), axis=1, keepdims=True)
    visible = (segment_rows == own_segment) & (column <= own) & (column + first >= 0) & (column >= 1)
    visible = visible[:, :span]

    scores = lax.dot_general(
        queries, keys, (((1,), (1,)), ((), ())), preferred_element_type=F32
    ) * HEAD_DIM ** (-0.5)
    scores = scores.reshape(Q_HEADS, rows, span)
    scores = jnp.where(visible[None], scores, F32(-1e30))
    highest = jnp.max(scores, axis=-1, keepdims=True)
    exponentials = jnp.where(visible[None], jnp.exp(scores - highest), F32(0.0))
    totals = jnp.sum(exponentials, axis=-1, keepdims=True)
    attention = (exponentials / totals).astype(BF16).reshape(Q_HEADS * rows, span)
    mixed = jnp.dot(attention, values, preferred_element_type=F32).astype(BF16)
    for h in range(Q_HEADS):
        piece = mixed[h * rows : (h + 1) * rows]
        for j in range(parts):
            out_ref[j, :, h * HEAD_DIM : (h + 1) * HEAD_DIM] = piece


def output_kernel(x_ref, mixed_ref, weight_ref, out_ref):
    product = jnp.dot(mixed_ref[...], weight_ref[...], preferred_element_type=F32)
    out_ref[...] = (x_ref[...].astype(F32) + product).astype(BF16)


VMEM = pl.BlockSpec(memory_space=pltpu.VMEM)
ANY = pl.BlockSpec(memory_space=pl.ANY)
PARAMS = pltpu.CompilerParams(vmem_limit_bytes=24 * 1024 * 1024)


def shard(shape):
    return jax.ShapeDtypeStruct(shape, BF16)


def exchange(value):
    return lax.all_to_all(value, "tp", split_axis=0, concat_axis=0, tiled=True)


def attend(segments, got, width, back, waited=()):
    parts, rows, _ = got.shape
    return pl.pallas_call(
        functools.partial(attend_kernel, parts, width, back),
        out_shape=shard((parts, rows, Q_COLS)),
        in_specs=[VMEM, VMEM] + [ANY] * len(waited),
        out_specs=VMEM,
        compiler_params=PARAMS,
        name="attend",
    )(segments, got, *waited)


def project_out(current, mixed, out_weight):
    return pl.pallas_call(
        output_kernel,
        out_shape=shard(current.shape),
        in_specs=[VMEM] * 3,
        out_specs=VMEM,
        compiler_params=PARAMS,
        name="project_out",
    )(current, mixed.reshape(current.shape[0], Q_COLS), out_weight)


def shards(carried, fresh, gains, qkv_weight, out_weight, segments, evict_tick):
    sections = lax.axis_size("pipe")
    parts = lax.axis_size("tp")
    ticks = fresh.shape[0] + 1
    tokens, width = carried.shape[1:]
    rows = tokens // parts
    columns = Q_COLS + window_blocks(rows) * KV_COLS
    following = [(i, i + 1) for i in range(sections - 1)]
    half = sections // 2
    across = [(i, i + half) for i in range(half)]
    turned = [(i, half - 1 - i) for i in range(half)]
    turned_across = [(half + i, sections - 1 - i) for i in range(half)]
    inputs = [carried[0]]
    for tick in range(ticks):
        outs = [shard((parts, rows, columns))]
        operands = [inputs[0], gains, qkv_weight[0]]
        specs = [VMEM] * 3
        if tick > 0:
            arrived = lax.ppermute(result, "pipe", following)
            operands = [arrived, fresh, gains, qkv_weight[0]]
            specs = [VMEM] * 4
            outs.append(shard((tokens, width)))
        if tick == ticks - 1:
            operands[:0] = [jnp.broadcast_to(evict_tick, (8, 128)), *inputs]
            specs[:0] = [VMEM] * (tick + 1)
            outs += [shard((tokens // 2, width))] * 2
        got = pl.pallas_call(
            functools.partial(project_kernel, parts, tick, tick == ticks - 1),
            out_shape=outs,
            in_specs=specs,
            out_specs=[VMEM] * len(outs),
            compiler_params=PARAMS,
            name="project",
        )(*operands)
        partial_proj = got[0]
        if tick > 0:
            inputs.append(got[1])
        sums = exchange(partial_proj)
        waited = ()
        if tick == ticks - 1:
            waited = (lax.ppermute(got[2], "pipe", across), lax.ppermute(got[3], "pipe", turned))
        mixed = exchange(attend(segments, sums, width * parts, ticks - 1 - tick, waited))
        result = project_out(inputs[tick], mixed, out_weight[0])
    top = lax.ppermute(waited[0], "pipe", turned_across)
    low = lax.ppermute(waited[1], "pipe", across)
    evicted = jnp.concatenate([top, low], axis=0)
    return (result[None], evicted[None])


def solution(mesh):
    placed = (
        P("pipe", None, "tp"),
        P(None, None, "tp"),
        P("pipe", "tp"),
        P("pipe", "tp", None),
        P("pipe", None, "tp"),
        P(),
        P("pipe"),
    )
    return jax.shard_map(
        shards,
        mesh=mesh,
        in_specs=placed,
        out_specs=(P("pipe", None, "tp"), P("pipe", None, "tp")),
        check_vma=False,
    )
```
